256 devices in a mesh: view: 2 (over x_hi), row: 4 (over x_lo, core), col: 32 (over y, z).
Axes of the slice: x: 4 (x_hi: 2, x_lo: 2; x = x_hi * 2 + x_lo), y: 4, z: 8, core: 2. Of those that a mesh axis runs over, the one named last changes fastest.
Arguments:
- image: float32 [2, 32, 32768], P('view', 'row', 'col'), may hold values from -6 to 6
- coarse: int32 [2, 32, 32768], P('view', 'row', 'col'), may hold values from 0 to 512, as said below
- bounds: int32 [2, 4, 32, 2], P('view', 'row', 'col'), may hold values from 0 to 512, as said below
Outputs:
- refinement: float32 [2, 32, 32768], P('view', 'row', 'col')
- dual: float32 [2, 2, 32, 32768], P('view', None, 'row', 'col')
The draws below stay inside these ranges and needn't reach their ends.
Inputs may be any that keep to these rules, and one draw needn't show every extreme that they name: `bounds`: for each view and tile the lower bound is under the upper bound, the lower bound is at most 255 and the upper at least 256; some tile has upper bound 512 and some has lower bound 0. Every pixel's coarse disparity lies within its tile's bounds; both ends of the range are reached.
All inputs are finite; a program needn't handle non-finite values.
Results may differ from the reference program's by a relative error of at most 0.000088.
Values sent between devices are 32-bit elements; how exact they have to be, the bound alone decides.
No kernel may reach another device: no remote copies, remote signals or barrier semaphores. Data moves between devices by JAX's collectives and lax.ppermute only.
A program may use at most 64 MiB of HBM per device.

```python
import jax
import jax.numpy as jnp

VIEWS = 2
DMAX = 512
ITERS = 4
TILE_ROWS = 8
TILE_COLS = 1024
ROWS = 32
COLS = 32768
N_ROW = 4
N_COL = 32


def tile_bounds(key):
    first, second = jax.random.split(key)
    low_bound = jax.random.randint(first, (VIEWS, N_ROW, N_COL), 0, DMAX // 2)
    spread_width = jax.random.randint(second, (VIEWS, N_ROW, N_COL), DMAX // 2, DMAX + 1)
    high_bound = jnp.minimum(low_bound + spread_width, DMAX)
    low_bound = low_bound.at[1, 0, 0].set(0)
    high_bound = high_bound.at[0, 0, 0].set(DMAX)
    return (low_bound, high_bound)


def draw_bounds(key, part):
    low_bound, high_bound = tile_bounds(key)
    return jnp.stack([low_bound, high_bound], axis=-1).astype(jnp.int32)


def draw_coarse(key, part):
    low_bound, high_bound = tile_bounds(key)
    key = jax.random.fold_in(key, 5)
    low_pixel = jnp.repeat(jnp.repeat(low_bound, TILE_ROWS, axis=1), TILE_COLS, axis=2)
    high_pixel = jnp.repeat(jnp.repeat(high_bound, TILE_ROWS, axis=1), TILE_COLS, axis=2)
    offsets = jax.random.randint(key, (VIEWS, ROWS, COLS), low_pixel, high_pixel + 1)
    offsets = offsets.at[0, 0, 0].set(DMAX).at[1, 0, 0].set(0)
    return offsets.astype(jnp.int32)


def block_scale(own_key, shape, shards, low, largest):
    def one(axis_at, blocks):
        heights = jax.random.uniform(jax.random.fold_in(jax.random.fold_in(own_key, 6), axis_at), (blocks,), jnp.float32, low / len(shards), largest / len(shards))
        return jnp.repeat(jnp.exp(heights), shape[axis_at] // blocks).reshape((-1,) + (1,) * (len(shape) - axis_at - 1))

    level = one(*shards[0])
    for cut in shards[1:]:
        level = level * one(*cut)
    return level


def centred(key, dims, deviation, bound, cuts=(), kind=jnp.bfloat16):
    entries = deviation * jax.random.normal(key, dims, jnp.float32)
    if cuts:
        entries = entries * block_scale(key, dims, cuts, -0.22, 0.18)
    return jnp.clip(entries, -bound, bound).astype(kind)


def setup_inputs(seed: int = 0) -> dict:
    key_of = jax.random.split(jax.random.key(seed), 4)
    image = centred(key_of[0], (VIEWS, ROWS, COLS), 1.0, 6.0, ((0, 2), (1, 4), (2, 32)), jnp.float32)
    coarse = draw_coarse(jax.random.fold_in(key_of[3], 71), 0)
    bounds = draw_bounds(jax.random.fold_in(key_of[3], 71), 0)
    return {"image": image, "coarse": coarse, "bounds": bounds}


data_weight = 1.0
couple_weight = 0.5
tau_step = 0.25
sigma_step = 0.5
huber_eps = 0.05
edge_gain = 2.0
slope_floor = 0.05

def forward_across(field):
    diff = field[:, :, 1:] - field[:, :, :-1]
    return jnp.concatenate([diff, jnp.zeros_like(field[:, :, :1])], axis=2)

def forward_down(field):
    diff = field[:, 1:, :] - field[:, :-1, :]
    return jnp.concatenate([diff, jnp.zeros_like(field[:, :1, :])], axis=1)

def behind_across(field):
    return jnp.concatenate([jnp.zeros_like(field[:, :, :1]), field[:, :, :-1]], axis=2)

def behind_down(field):
    return jnp.concatenate([jnp.zeros_like(field[:, :1, :]), field[:, :-1, :]], axis=1)

def tile_spread(values):
    return jnp.repeat(jnp.repeat(values, TILE_ROWS, axis=1), TILE_COLS, axis=2)

def reference(image, coarse, bounds):
    direction = jnp.array([1, -1], dtype=jnp.int32)[:, None, None]
    direction_real = direction.astype(image.dtype)
    pad_width = DMAX + 1
    col_index = jnp.arange(COLS, dtype=jnp.int32)[None, None, :]
    target = col_index - direction * coarse
    pick_col = (target + pad_width).astype(jnp.int32)
    inside = ((target >= 0) & (target < COLS)).astype(image.dtype)
    offset_real = coarse.astype(image.dtype)
    lower_bound = tile_spread(bounds[..., 0]).astype(image.dtype)
    upper_bound = tile_spread(bounds[..., 1]).astype(image.dtype)

    def warp(field, shift):
        padded = jnp.pad(field[::-1], ((0, 0), (0, 0), (pad_width, pad_width)))
        return jnp.take_along_axis(padded, pick_col + shift, axis=2)
    warped = warp(image, 0)
    slope_data = -direction_real * (warp(image, 1) - warp(image, -1)) * 0.5
    residue = warped - image
    grad_across = forward_across(image)
    grad_down = forward_down(image)
    edge_weight = 1.0 / (1.0 + edge_gain * (grad_across * grad_across + grad_down * grad_down))
    couple = couple_weight * inside
    blend_denom = 1.0 + tau_step * couple
    clip_limit = data_weight * tau_step / blend_denom
    primal = offset_real
    relaxed = primal
    dual_across = jnp.zeros_like(image)
    dual_down = jnp.zeros_like(image)
    for sweep in range(ITERS):
        trial_across = (dual_across + sigma_step * forward_across(relaxed)) / (1.0 + sigma_step * huber_eps)
        trial_down = (dual_down + sigma_step * forward_down(relaxed)) / (1.0 + sigma_step * huber_eps)
        shrink = jnp.sqrt(jnp.maximum(1.0, (trial_across * trial_across + trial_down * trial_down) / (edge_weight * edge_weight)))
        dual_across = trial_across / shrink
        dual_down = trial_down / shrink
        diverge = dual_across - behind_across(dual_across) + dual_down - behind_down(dual_down)
        partner = warp(primal, 0)
        blended = (primal + tau_step * diverge + tau_step * couple * partner) / blend_denom
        mismatch = residue + slope_data * (blended - offset_real)
        update_step = jnp.clip(mismatch / jnp.maximum(slope_data * slope_data, slope_floor), -clip_limit, clip_limit)
        refined = jnp.clip(blended - slope_data * update_step, lower_bound, upper_bound)
        relaxed = 2.0 * refined - primal
        primal = refined
    return (primal - offset_real, jnp.stack([dual_across, dual_down], axis=1))
```

```python
import jax
import jax.numpy as jnp
from jax import lax
from jax.experimental import pallas as pl
from jax.experimental.pallas import tpu as pltpu
from jax.sharding import PartitionSpec as P

AXES = ("view", "row", "col")
LANES = 128
OUT_ROWS = 8
BLOCKS = 8
TILE_PACK = 17
STRIP = 32
SHIFT = 10
WIDE = 40
TALL = 16
VMEM_BYTES = 40 * 1024 * 1024

tau = 0.25
sigma = 0.5
huber_eps = 0.05
edge_gain = 2.0
slope_floor = 0.05
couple_weight = 0.5
data_weight = 1.0


def swapped(block, partner, sizes):
    views, rows, cols = sizes
    route = []
    for v in range(views):
        for r in range(rows):
            for c in range(cols):
                to_v, to_r, to_c = partner(v, r, c)
                if 0 <= to_r < rows and 0 <= to_c < cols:
                    route.append(((v * rows + r) * cols + c, (to_v * rows + to_r) * cols + to_c))
    return lax.ppermute(block, AXES, route)


def to_slabs(tile):
    parts = jnp.stack([tile[:, LANES * j : LANES * (j + 1)] for j in range(BLOCKS)])
    return jnp.transpose(parts, (1, 0, 2))


def pack_kernel(image_ref, coarse_ref, bounds_ref, out_ref):
    out_ref[0:8] = to_slabs(image_ref[0])
    out_ref[8:16] = to_slabs(coarse_ref[0].astype(jnp.float32))
    sub = lax.broadcasted_iota(jnp.int32, (BLOCKS, LANES), 0)
    out_ref[16] = jnp.where(sub == 0, bounds_ref[0, 0], bounds_ref[0, 1]).astype(jnp.float32)


def join_kernel(own_ref, other_ref, both_ref, first_ref, second_ref):
    lower = ((lax.axis_index("col") >> 1) & 1) == 0
    both_ref[0:TILE_PACK] = own_ref[...]
    both_ref[TILE_PACK : 2 * TILE_PACK] = other_ref[...]
    for w, ref in enumerate((own_ref, other_ref)):
        for i in range(16):
            head, tail = ref[i, 0:1, :], ref[i, 7:8, :]
            at = w * 16 + i
            first_ref[at : at + 1, :] = jnp.where(lower, tail, head)
            second_ref[at : at + 1, :] = jnp.where(lower, head, tail)


def assemble_kernel(both_ref, a_ref, b_ref, thin1_ref, thin2_ref, m1_ref, m2_ref):
    col, row = lax.axis_index("col"), lax.axis_index("row")
    odd = (col & 1) == 1
    upper = ((col >> 1) & 1) == 1
    even_row = (row & 1) == 0
    thin_left = jnp.where(upper, thin1_ref[...], thin2_ref[...])
    thin_right = jnp.where(upper, thin2_ref[...], thin1_ref[...])

    def put(plane, y, at, top, bottom):
        n = top.shape[0]
        m1_ref[plane, y, at : at + n, :] = jnp.where(even_row, bottom, top)
        m2_ref[plane, y, at : at + n, :] = jnp.where(even_row, top, bottom)

    for plane in range(4):
        w, kind = plane // 2, plane % 2
        base = w * TILE_PACK + kind * 8
        for y in range(4):
            t, b = base + y, base + y + 4
            at, ab = plane * 8 + y, plane * 8 + y + 4
            put(plane, y, 0, thin_left[at : at + 1], thin_left[ab : ab + 1])
            put(plane, y, 1, jnp.where(odd, a_ref[t], b_ref[t]), jnp.where(odd, a_ref[b], b_ref[b]))
            put(plane, y, 9, both_ref[t], both_ref[b])
            put(plane, y, 17, jnp.where(odd, b_ref[t], a_ref[t]), jnp.where(odd, b_ref[b], a_ref[b]))
            put(plane, y, 25, thin_right[at : at + 1], thin_right[ab : ab + 1])
            if kind == 0 and y == 0:
                s = w * TILE_PACK + 16
                left = jnp.where(odd, a_ref[s, 0:2], b_ref[s, 0:2])
                right = jnp.where(odd, b_ref[s, 0:2], a_ref[s, 0:2])
                put(plane, y, 26, left, left)
                put(plane, y, 28, both_ref[s, 0:2], both_ref[s, 0:2])
                put(plane, y, 30, right, right)
            else:
                zero = jnp.zeros((6, LANES), jnp.float32)
                put(plane, y, 26, zero, zero)


def plans(view):
    if view == 0:
        other = (((-9, -1, 4), (-8, 0, 4)), ((-5, 1), (-5, 1)), ((-5, 0), (-4, 0)), None)
        slopes = ((-8, 0, 8), (-9, -1, 5))
    else:
        other = (((-5, 3, 8), (-4, 4, 8)), ((-1, 5), (-1, 5)), ((-1, 4), (0, 4)), None)
        slopes = ((-8, 0, 8), (-5, 3, 9))
    own = (((-5, 3, 5), (-5, 3, 5)), ((-5, 3, 4), (-4, 4)), ((-1, 1), (-1, 1)), ((-1, 0), (0,)))
    return own, other, slopes


def refine_kernel(sizes, m1_ref, m2_ref, g1_ref, g2_ref, refine_ref, dual_ref, *scratch):
    (F, G, D, RES, SL, INV, RD, IE, LO, HI, UA, UB, RA, RB, XA, XB, YA, YB, MX, CV, XG, OUT) = scratch
    _, n_row, n_col = sizes
    view, row, col = lax.axis_index("view"), lax.axis_index("row"), lax.axis_index("col")
    even_row = (row & 1) == 0
    lane = lax.broadcasted_iota(jnp.int32, (8, LANES), 1)
    sub = lax.broadcasted_iota(jnp.int32, (8, LANES), 0)
    total = n_col * BLOCKS * LANES

    for plane in range(4):
        for y in range(4):
            for at in (0, 8, 16, 24):
                n = 2 if at == 24 else 8
                m1, m2 = m1_ref[plane, y, at : at + n], m2_ref[plane, y, at : at + n]
                g1, g2 = g1_ref[plane, y, at : at + n], g2_ref[plane, y, at : at + n]
                to = slice(at + 1, at + 1 + n)
                F[plane, y, to] = jnp.where(even_row, g2, g1)
                F[plane, y + 4, to] = jnp.where(even_row, m2, m1)
                F[plane, y + 8, to] = jnp.where(even_row, m1, m2)
                F[plane, y + 12, to] = jnp.where(even_row, g1, g2)
        for y in range(TALL):
            F[plane, y, 0:1] = jnp.zeros((1, LANES), jnp.float32)
            F[plane, y, 27:40] = jnp.zeros((13, LANES), jnp.float32)
    for w in range(2):
        above = jnp.where(even_row, g2_ref[2 * w, 0, 26:32], g1_ref[2 * w, 0, 26:32])
        below = jnp.where(even_row, g1_ref[2 * w, 0, 26:32], g2_ref[2 * w, 0, 26:32])
        for rg, rows in enumerate((above, m1_ref[2 * w, 0, 26:32], below)):
            for j in range(3):
                at = SHIFT - 8 + 8 * j
                LO[w, rg, at : at + 8] = jnp.broadcast_to(rows[2 * j : 2 * j + 1], (8, LANES))
                HI[w, rg, at : at + 8] = jnp.broadcast_to(rows[2 * j + 1 : 2 * j + 2], (8, LANES))
            LO[w, rg, 26:40] = jnp.zeros((14, LANES), jnp.float32)
            HI[w, rg, 26:40] = jnp.zeros((14, LANES), jnp.float32)
            LO[w, rg, 0:2] = jnp.zeros((2, LANES), jnp.float32)
            HI[w, rg, 0:2] = jnp.zeros((2, LANES), jnp.float32)
    for i in range(0, WIDE, 8):
        x = (col * BLOCKS + (i - SHIFT) + sub) * LANES
        XG[i : i + 8] = x
        valid = (x >= 0) & (x < total)
        CV[i : i + 8] = jnp.where(valid, 1.0, 0.0)
        MX[i : i + 8] = jnp.where(valid & (x + lane < total - 1), 1.0, 0.0)

    def ahead(ref, lead, i):
        here, after = ref[(*lead, pl.ds(i, 8))], ref[(*lead, pl.ds(i + 1, 8))]
        return here, pltpu.roll(jnp.where(lane == 0, after, here), LANES - 1, 1)

    def behind(ref, lead, i):
        here, before = ref[(*lead, pl.ds(i, 8))], ref[(*lead, pl.ds(i - 1, 8))]
        return here, pltpu.roll(jnp.where(lane == LANES - 1, before, here), 1, 1)

    def masks(ry):
        y = row * OUT_ROWS + ry - 4
        ok = jnp.where((y >= 0) & (y < n_row * OUT_ROWS), 1.0, 0.0)
        down = jnp.where((y >= 0) & (y < n_row * OUT_ROWS - 1), 1.0, 0.0)
        return ok, down

    def dual_step(k, w, ry, starts, ubar, p_in, p_out):
        ok, down = masks(ry)
        for g in starts:
            i = g + SHIFT
            mx = MX[i : i + 8] * ok
            my = CV[i : i + 8] * down
            if k == 0:
                here, right = ahead(F, (2 * w, ry), i)
                gx, gy = (right - here) * mx, (F[2 * w, ry + 1, pl.ds(i, 8)] - here) * my
                inverse = 1.0 + edge_gain * (gx * gx + gy * gy)
                ie = inverse * inverse
                IE[w, ry, pl.ds(i, 8)] = ie
            else:
                ie = IE[w, ry, pl.ds(i, 8)]
            lead = (2 * w + 1, ry) if k == 0 else (w, ry)
            lead_down = (2 * w + 1, ry + 1) if k == 0 else (w, ry + 1)
            here, right = ahead(ubar, lead, i)
            gx = (right - here) * mx
            gy = (ubar[(*lead_down, pl.ds(i, 8))] - here) * my
            if k == 0:
                qx, qy = sigma * gx, sigma * gy
            else:
                qx = p_in[0][w, ry, pl.ds(i, 8)] + sigma * gx
                qy = p_in[1][w, ry, pl.ds(i, 8)] + sigma * gy
            qx, qy = qx * (1.0 / (1.0 + sigma * huber_eps)), qy * (1.0 / (1.0 + sigma * huber_eps))
            shrink = lax.rsqrt(jnp.maximum(1.0, (qx * qx + qy * qy) * ie))
            p_out[0][w, ry, pl.ds(i, 8)] = qx * shrink
            p_out[1][w, ry, pl.ds(i, 8)] = qy * shrink

    def primal_step(k, w, sign, ry, starts, u_in, p_out, u_out, ubar_out):
        ok, _ = masks(ry)
        rg = (ry >= 4).astype(jnp.int32) + (ry >= 12).astype(jnp.int32)
        for g in starts:
            i = g + SHIFT
            here = pl.ds(i, 8)
            d0 = F[2 * w + 1, ry, here]
            if k == 0:
                t = lane - sign * d0.astype(jnp.int32)
                D[w, ry, here] = t
            else:
                t = D[w, ry, here]
            place, hop = t & (LANES - 1), t >> 7
            picks = [hop == -sign * m for m in range(1, 5)]

            def read(ref, lead):
                value = jnp.take_along_axis(ref[(*lead, here)], place, axis=1)
                for m in range(1, 5):
                    more = jnp.take_along_axis(ref[(*lead, pl.ds(i - sign * m, 8))], place, axis=1)
                    value = jnp.where(picks[m - 1], more, value)
                return value

            if k == 0:
                residue = read(F, (2 * (1 - w), ry)) - F[2 * w, ry, here]
                slope = read(G, (1 - w, ry)) * float(-sign)
                inv = 1.0 / jnp.maximum(slope * slope, slope_floor)
                target = XG[i : i + 8] + t
                inside = (target >= 0) & (target < total)
                rden = jnp.where(inside, 1.0 / (1.0 + tau * couple_weight), 1.0)
                if k + 1 < 4:
                    RES[w, ry, here] = residue
                    SL[w, ry, here] = slope
                    INV[w, ry, here] = inv
                    RD[w, ry, here] = rden
            else:
                residue, slope = RES[w, ry, here], SL[w, ry, here]
                inv, rden = INV[w, ry, here], RD[w, ry, here]
            partner = read(u_in, (2 * (1 - w) + 1, ry) if k == 0 else (1 - w, ry))
            u = d0 if k == 0 else u_in[w, ry, here]
            px, px_left = behind(p_out[0], (w, ry), i)
            div = px - px_left + p_out[1][w, ry, here] - p_out[1][w, ry - 1, here]
            blended = (u + tau * div + (tau * couple_weight) * partner) * rden
            mismatch = residue + slope * (blended - d0)
            limit = (data_weight * tau) * rden
            step = jnp.minimum(jnp.maximum(mismatch * inv, -limit), limit)
            new = jnp.minimum(jnp.maximum(blended - slope * step, LO[w, rg, here]), HI[w, rg, here])
            if k < 3:
                new = new * (CV[i : i + 8] * ok)
                u_out[w, ry, here] = new
                ubar_out[w, ry, here] = 2.0 * new - u
            else:
                OUT[ry - 4] = new - d0

    def run(v):
        own, other, slopes = plans(v)
        signs = (1 - 2 * v, 2 * v - 1)

        def slope_row(ry, carry):
            for w in range(2):
                for g in slopes[w]:
                    i = g + SHIFT
                    _, right = ahead(F, (2 * w, ry), i)
                    _, left = behind(F, (2 * w, ry), i)
                    G[w, ry, pl.ds(i, 8)] = (right - left) * 0.5
            return carry

        lax.fori_loop(1, 15, slope_row, 0)
        u_bufs = (F, UA, UB, UA, None)
        ubar_bufs = (F, RA, RB, RA, None)
        p_bufs = (None, (XA, YA), (XB, YB), (XA, YA), (XB, YB))
        for k in range(4):
            first, last = k + 1, 15 - k

            def dual_row(ry, k=k):
                for w, plan in enumerate((own, other)):
                    if plan[k] is not None:
                        dual_step(k, w, ry, plan[k][0], ubar_bufs[k], p_bufs[k], p_bufs[k + 1])

            def body(ry, carry, k=k, dual_row=dual_row):
                dual_row(ry)
                for w, plan in enumerate((own, other)):
                    if plan[k] is not None:
                        primal_step(k, w, signs[w], ry, plan[k][1], u_bufs[k], p_bufs[k + 1], u_bufs[k + 1], ubar_bufs[k + 1])
                return carry

            dual_row(first - 1)
            lax.fori_loop(first, last, body, 0)

    @pl.when(view == 0)
    def _():
        run(0)

    @pl.when(view == 1)
    def _():
        run(1)

    def from_slabs(slabs, put):
        parts = jnp.transpose(slabs, (1, 0, 2))
        for j in range(BLOCKS):
            put(slice(LANES * j, LANES * (j + 1)), parts[j])

    def put_refine(at, value):
        refine_ref[0, :, at] = value

    def put_x(at, value):
        dual_ref[0, 0, :, at] = value

    def put_y(at, value):
        dual_ref[0, 1, :, at] = value

    from_slabs(OUT[...], put_refine)
    from_slabs(XB[0, 4:12, SHIFT : SHIFT + 8], put_x)
    from_slabs(YB[0, 4:12, SHIFT : SHIFT + 8], put_y)


def on_device(sizes, image, coarse, bounds):
    f32 = jnp.float32
    vmem = pl.BlockSpec(memory_space=pltpu.VMEM)
    smem = pl.BlockSpec(memory_space=pltpu.SMEM)
    params = pltpu.CompilerParams(vmem_limit_bytes=VMEM_BYTES)
    own = pl.pallas_call(
        pack_kernel,
        out_shape=jax.ShapeDtypeStruct((TILE_PACK, BLOCKS, LANES), f32),
        in_specs=[vmem, vmem, smem],
        out_specs=vmem,
        compiler_params=params,
    )(image, coarse, bounds.reshape(1, 2))
    other = swapped(own, lambda v, r, c: (1 - v, r, c), sizes)
    thin_shape = jax.ShapeDtypeStruct((32, LANES), f32)
    both, thin1, thin2 = pl.pallas_call(
        join_kernel,
        out_shape=(jax.ShapeDtypeStruct((2 * TILE_PACK, BLOCKS, LANES), f32), thin_shape, thin_shape),
        in_specs=[vmem, vmem],
        out_specs=(vmem, vmem, vmem),
        compiler_params=params,
    )(own, other)
    side_b = swapped(both, lambda v, r, c: (v, r, ((c + 1) ^ 1) - 1), sizes)
    side_a = swapped(both, lambda v, r, c: (v, r, c ^ 1), sizes)
    thin2 = swapped(thin2, lambda v, r, c: (v, r, ((c + 2) ^ 2) - 2), sizes)
    thin1 = swapped(thin1, lambda v, r, c: (v, r, c ^ 2), sizes)
    strip = jax.ShapeDtypeStruct((4, 4, STRIP, LANES), f32)
    m1, m2 = pl.pallas_call(
        assemble_kernel,
        out_shape=(strip, strip),
        in_specs=[vmem] * 5,
        out_specs=(vmem, vmem),
        compiler_params=params,
    )(both, side_a, side_b, thin1, thin2)
    g2 = swapped(m2, lambda v, r, c: (v, ((r + 1) ^ 1) - 1, c), sizes)
    g1 = swapped(m1, lambda v, r, c: (v, r ^ 1, c), sizes)

    def field(n, dtype=f32):
        return pltpu.VMEM((n, TALL, WIDE, LANES), dtype)

    scratch = [field(4), field(2), field(2, jnp.int32)]
    scratch += [field(2) for _ in range(5)]
    scratch += [pltpu.VMEM((2, 3, WIDE, LANES), f32) for _ in range(2)]
    scratch += [field(2) for _ in range(8)]
    scratch += [pltpu.VMEM((WIDE, LANES), f32), pltpu.VMEM((WIDE, LANES), f32), pltpu.VMEM((WIDE, LANES), jnp.int32)]
    scratch += [pltpu.VMEM((OUT_ROWS, BLOCKS, LANES), f32)]
    refine, dual = pl.pallas_call(
        lambda *refs: refine_kernel(sizes, *refs),
        out_shape=(
            jax.ShapeDtypeStruct((1, OUT_ROWS, BLOCKS * LANES), f32),
            jax.ShapeDtypeStruct((1, 2, OUT_ROWS, BLOCKS * LANES), f32),
        ),
        in_specs=[vmem] * 4,
        out_specs=(vmem, vmem),
        scratch_shapes=scratch,
        compiler_params=params,
    )(m1, m2, g1, g2)
    return refine, dual


def solution(mesh):
    sizes = tuple(mesh.shape[axis] for axis in AXES)
    return jax.shard_map(
        lambda *args: on_device(sizes, *args),
        mesh=mesh,
        in_specs=(P("view", "row", "col"), P("view", "row", "col"), P("view", "row", "col", None)),
        out_specs=(P("view", "row", "col"), P("view", None, "row", "col")),
        check_vma=False,
    )
```

```python
import jax
import jax.numpy as jnp
from jax import lax
from jax.experimental import pallas as pl
from jax.experimental.pallas import tpu as pltpu
from jax.sharding import PartitionSpec as P

AXES = ("view", "row", "col")
LANES = 128
OUT_ROWS = 8
BLOCKS = 8
TILE_PACK = 17
STRIP = 36
SHIFT = 16
WIDE = 40
TALL = 16
VMEM_BYTES = 40 * 1024 * 1024

tau = 0.25
sigma = 0.5
huber_eps = 0.05
edge_gain = 2.0
slope_floor = 0.05
couple_weight = 0.5
data_weight = 1.0


def swapped(block, partner, sizes):
    views, rows, cols = sizes
    route = []
    for v in range(views):
        for r in range(rows):
            for c in range(cols):
                to_v, to_r, to_c = partner(v, r, c)
                if 0 <= to_r < rows and 0 <= to_c < cols:
                    route.append(((v * rows + r) * cols + c, (to_v * rows + to_r) * cols + to_c))
    return lax.ppermute(block, AXES, route)


def to_slabs(tile):
    parts = jnp.stack([tile[:, LANES * j : LANES * (j + 1)] for j in range(BLOCKS)])
    return jnp.transpose(parts, (1, 0, 2))


def pack_kernel(image_hbm, coarse_hbm, bounds_hbm, out_ref, edge_ref, image_ref, coarse_ref, bounds_ref, sems):
    copies = [
        pltpu.make_async_copy(source, target, sems.at[n])
        for n, (source, target) in enumerate(
            ((image_hbm, image_ref), (coarse_hbm, coarse_ref), (bounds_hbm, bounds_ref))
        )
    ]
    for copy in copies:
        copy.start()
    odd = (lax.axis_index("col") & 1) == 1
    last = (BLOCKS - 1) * LANES
    copies[0].wait()
    image = image_ref[0]
    out_ref[0:8] = to_slabs(image)
    edge_ref[0] = jnp.where(odd, image[:, :LANES], image[:, last:])
    copies[1].wait()
    coarse = coarse_ref[0].astype(jnp.float32)
    out_ref[8:16] = to_slabs(coarse)
    edge_ref[1] = jnp.where(odd, coarse[:, :LANES], coarse[:, last:])
    copies[2].wait()
    sub = lax.broadcasted_iota(jnp.int32, (BLOCKS, LANES), 0)
    out_ref[16] = jnp.where(sub == 0, bounds_ref[0, 0, 0, 0], bounds_ref[0, 0, 0, 1]).astype(jnp.float32)


def join_kernel(own_ref, other_ref, edge_own_ref, edge_other_ref, both_ref, more_ref):
    for ref in (both_ref, more_ref):
        ref[0:TILE_PACK] = own_ref[...]
        ref[TILE_PACK : 2 * TILE_PACK] = other_ref[...]
    more_ref[2 * TILE_PACK] = edge_own_ref[0]
    more_ref[2 * TILE_PACK + 1 :] = edge_other_ref[...]


def near_kernel(b_ref, out_ref):
    odd = (lax.axis_index("col") & 1) == 1
    for n, base in enumerate((0, TILE_PACK, TILE_PACK + 8)):
        for y in range(8):
            out_ref[n, y : y + 1, :] = jnp.where(odd, b_ref[base + y, 0:1], b_ref[base + y, 7:8])


def halo_slabs(view):
    mid = (-5, 1) if view == 0 else (-1, 5)
    slabs = [(p, d, g) for p in (0, 1) for d in (1, 2) for g in (-8, 0, 8)]
    slabs += [(p, d, g) for p in (0, 1) for d in (3, 4) for g in (-1, 1)]
    slabs += [(p, 1, g) for p in (2, 3) for g in (-8, 0, 8)]
    slabs += [(p, d, g) for p in (2, 3) for d in (2, 3) for g in mid]
    return slabs


def assemble_kernel(both_ref, a_ref, b_ref, far_ref, m1_ref, m2_ref, F, LO, HI):
    odd = (lax.axis_index("col") & 1) == 1
    even_row = (lax.axis_index("row") & 1) == 0
    first = lax.axis_index("view") == 0
    zero = jnp.zeros((8, LANES), jnp.float32)
    for plane in range(4):
        base = (plane // 2) * TILE_PACK + (plane % 2) * 8
        for y in range(8):
            at = base + y
            F[plane, y + 4, 0:8] = zero
            F[plane, y + 4, 8:16] = jnp.where(odd, a_ref[at], b_ref[at])
            F[plane, y + 4, 16:24] = both_ref[at]
            F[plane, y + 4, 24:32] = jnp.where(odd, b_ref[at], a_ref[at])
            F[plane, y + 4, 32:40] = zero
    far, near = far_ref[...], b_ref[2 * TILE_PACK :]
    left, right = jnp.where(odd, far, near), jnp.where(odd, near, far)
    cross = jnp.where(first, left, right)
    low, high = SHIFT - 9, SHIFT + 16
    for y in range(8):
        row = slice(y, y + 1)
        F[0, y + 4, low : low + 1] = left[0, row]
        F[0, y + 4, high : high + 1] = right[0, row]
        for plane in (2, 3):
            F[plane, y + 4, low : low + 1] = cross[plane - 1, row]
            F[plane, y + 4, high : high + 1] = cross[plane - 1, row]

    def put(at, top, bottom):
        m1_ref[at] = jnp.where(even_row, bottom, top)
        m2_ref[at] = jnp.where(even_row, top, bottom)

    for at, ((plane, d, g), (_, _, g1)) in enumerate(zip(halo_slabs(0), halo_slabs(1), strict=True)):
        pair = []
        for ry in (3 + d, 12 - d):
            value = F[plane, ry, SHIFT + g : SHIFT + g + 8]
            if g1 != g:
                value = jnp.where(first, value, F[plane, ry, SHIFT + g1 : SHIFT + g1 + 8])
            pair.append(value)
        put(at, *pair)
    for w in range(2):
        s = w * TILE_PACK + 16
        tiles = (jnp.where(odd, a_ref[s], b_ref[s]), both_ref[s], jnp.where(odd, b_ref[s], a_ref[s]))
        thin = [jnp.concatenate([cross[1, y : y + 1], cross[2, y : y + 1]], axis=0) for y in (0, 7)]
        ends = [jnp.concatenate([t[0:2] for t in tiles] + [t], axis=0) for t in thin]
        put(STRIP - 2 + w, *ends)
        spread_bounds(LO, HI, w, 1, ends[0])


def spread_bounds(LO, HI, w, rg, rows):
    zero = jnp.zeros((8, LANES), jnp.float32)
    for j in range(3):
        at = SHIFT - 8 + 8 * j
        LO[w, rg, at : at + 8] = jnp.broadcast_to(rows[2 * j : 2 * j + 1], (8, LANES))
        HI[w, rg, at : at + 8] = jnp.broadcast_to(rows[2 * j + 1 : 2 * j + 2], (8, LANES))
    for ref in (LO, HI):
        ref[w, rg, 0:8] = zero
        ref[w, rg, 32:40] = zero


def plans(view):
    if view == 0:
        other_wide = (((-9, -1, 4), (-8, 0, 4)), ((-5, 1), (-5, 1)), ((-5, 0), (-4, 0)))
        other_narrow = ((-5, 1), (-5, 1))
        slope_wide, slope_narrow = (-9, -1, 5), (-5, 1)
    else:
        other_wide = (((-5, 3, 8), (-4, 4, 8)), ((-1, 5), (-1, 5)), ((-1, 4), (0, 4)))
        other_narrow = ((-1, 5), (-1, 5))
        slope_wide, slope_narrow = (-5, 3, 9), (-1, 5)
    own_wide = (((-5, 3, 5), (-5, 3, 5)), ((-5, 3, 4), (-4, 4)), ((-1, 1), (-1, 1)), ((-1, 0), (0,)))
    own_narrow = ((-1, 1), (-1, 1))
    return own_wide, own_narrow, other_wide, other_narrow, slope_wide, slope_narrow


def make_steps(sizes, state, MX, CV, XG, OUT):
    (F, LO, HI, G, D, RES, SL, INV, RD, IE, UA, RA, UB, RB, XA, YA, XB, YB) = state
    _, n_row, n_col = sizes
    view, row, col = lax.axis_index("view"), lax.axis_index("row"), lax.axis_index("col")
    lane = lax.broadcasted_iota(jnp.int32, (8, LANES), 1)
    sub = lax.broadcasted_iota(jnp.int32, (8, LANES), 0)
    total = n_col * BLOCKS * LANES
    u_bufs = (F, UA, UB, UA, None)
    ubar_bufs = (F, RA, RB, RA, None)
    p_bufs = (None, (XA, YA), (XB, YB), (XA, YA), (XB, YB))
    for i in range(0, WIDE, 8):
        x = (col * BLOCKS + (i - SHIFT) + sub) * LANES
        XG[i : i + 8] = x
        valid = (x >= 0) & (x < total)
        CV[i : i + 8] = jnp.where(valid, 1.0, 0.0)
        MX[i : i + 8] = jnp.where(valid & (x + lane < total - 1), 1.0, 0.0)

    def ahead(ref, lead, i):
        here, after = ref[(*lead, pl.ds(i, 8))], ref[(*lead, pl.ds(i + 1, 8))]
        return here, pltpu.roll(jnp.where(lane == 0, after, here), LANES - 1, 1)

    def behind(ref, lead, i):
        here, before = ref[(*lead, pl.ds(i, 8))], ref[(*lead, pl.ds(i - 1, 8))]
        return here, pltpu.roll(jnp.where(lane == LANES - 1, before, here), 1, 1)

    def masks(ry):
        y = row * OUT_ROWS + ry - 4
        ok = jnp.where((y >= 0) & (y < n_row * OUT_ROWS), 1.0, 0.0)
        down = jnp.where((y >= 0) & (y < n_row * OUT_ROWS - 1), 1.0, 0.0)
        return ok, down

    def dual_step(k, w, ry, starts, ubar, p_in, p_out, stores):
        ok, down = masks(ry)
        for g in starts:
            i = g + SHIFT
            mx = MX[i : i + 8] * ok
            my = CV[i : i + 8] * down
            here_at = (w, ry, pl.ds(i, 8))
            if k == 0:
                here, right = ahead(F, (2 * w, ry), i)
                gx, gy = (right - here) * mx, (F[2 * w, ry + 1, pl.ds(i, 8)] - here) * my
                inverse = 1.0 + edge_gain * (gx * gx + gy * gy)
                ie = inverse * inverse
                stores.append((IE, here_at, ie))
            else:
                ie = IE[here_at]
            lead = (2 * w + 1, ry) if k == 0 else (w, ry)
            lead_down = (2 * w + 1, ry + 1) if k == 0 else (w, ry + 1)
            here, right = ahead(ubar, lead, i)
            gx = (right - here) * mx
            gy = (ubar[(*lead_down, pl.ds(i, 8))] - here) * my
            if k == 0:
                qx, qy = sigma * gx, sigma * gy
            else:
                qx = p_in[0][here_at] + sigma * gx
                qy = p_in[1][here_at] + sigma * gy
            qx, qy = qx * (1.0 / (1.0 + sigma * huber_eps)), qy * (1.0 / (1.0 + sigma * huber_eps))
            shrink = lax.rsqrt(jnp.maximum(1.0, (qx * qx + qy * qy) * ie))
            stores.append((p_out[0], here_at, qx * shrink))
            stores.append((p_out[1], here_at, qy * shrink))

    def primal_step(k, w, sign, ry, starts, u_in, p_out, u_out, ubar_out, stores):
        ok, _ = masks(ry)
        rg = sum(int(ry >= n) if isinstance(ry, int) else (ry >= n).astype(jnp.int32) for n in (4, 12))
        for g in starts:
            i = g + SHIFT
            here = pl.ds(i, 8)
            here_at = (w, ry, here)
            d0 = F[2 * w + 1, ry, here]
            if k == 0:
                t = lane - sign * d0.astype(jnp.int32)
                stores.append((D, here_at, t))
            else:
                t = D[here_at]
            place, hop = t & (LANES - 1), t >> 7
            picks = [hop == -sign * m for m in range(1, 5)]

            def read(ref, lead):
                value = jnp.take_along_axis(ref[(*lead, here)], place, axis=1)
                for m in range(1, 5):
                    more = jnp.take_along_axis(ref[(*lead, pl.ds(i - sign * m, 8))], place, axis=1)
                    value = jnp.where(picks[m - 1], more, value)
                return value

            if k == 0:
                residue = read(F, (2 * (1 - w), ry)) - F[2 * w, ry, here]
                slope = read(G, (1 - w, ry)) * float(-sign)
                inv = 1.0 / jnp.maximum(slope * slope, slope_floor)
                target = XG[i : i + 8] + t
                inside = (target >= 0) & (target < total)
                rden = jnp.where(inside, 1.0 / (1.0 + tau * couple_weight), 1.0)
                stores += [(RES, here_at, residue), (SL, here_at, slope), (INV, here_at, inv), (RD, here_at, rden)]
            else:
                residue, slope = RES[here_at], SL[here_at]
                inv, rden = INV[here_at], RD[here_at]
            partner = read(u_in, (2 * (1 - w) + 1, ry) if k == 0 else (1 - w, ry))
            u = d0 if k == 0 else u_in[here_at]
            px, px_left = behind(p_out[0], (w, ry), i)
            div = px - px_left + p_out[1][here_at] - p_out[1][w, ry - 1, here]
            blended = (u + tau * div + (tau * couple_weight) * partner) * rden
            mismatch = residue + slope * (blended - d0)
            limit = (data_weight * tau) * rden
            step = jnp.minimum(jnp.maximum(mismatch * inv, -limit), limit)
            new = jnp.minimum(jnp.maximum(blended - slope * step, LO[w, rg, here]), HI[w, rg, here])
            if k < 3:
                new = new * (CV[i : i + 8] * ok)
                stores.append((u_out, here_at, new))
                stores.append((ubar_out, here_at, 2.0 * new - u))
            else:
                stores.append((OUT, (ry - 4,), new - d0))

    def slope_step(w, ry, starts, stores):
        for g in starts:
            i = g + SHIFT
            _, right = ahead(F, (2 * w, ry), i)
            _, left = behind(F, (2 * w, ry), i)
            stores.append((G, (w, ry, pl.ds(i, 8)), (right - left) * 0.5))

    def dual(k, w, y, starts, stores):
        dual_step(k, w, y + 4, starts, ubar_bufs[k], p_bufs[k], p_bufs[k + 1], stores)

    def primal(k, w, y, sign, starts, stores):
        primal_step(k, w, sign, y + 4, starts, u_bufs[k], p_bufs[k + 1], u_bufs[k + 1], ubar_bufs[k + 1], stores)

    def slopes(w, y, starts, stores):
        slope_step(w, y + 4, starts, stores)

    return dual, primal, slopes


def flush(stores):
    for ref, at, value in stores:
        ref[at] = value


def by_view(run):
    view = lax.axis_index("view")

    @pl.when(view == 0)
    def _():
        run(0)

    @pl.when(view == 1)
    def _():
        run(1)


def inner_kernel(sizes, F, LO, HI, *refs):
    state, (MX, CV, XG) = (F, LO, HI, *refs[:15]), refs[15:]
    dual, primal, slopes = make_steps(sizes, state, MX, CV, XG, None)

    def run(v):
        own, _, other, _, slope_other, _ = plans(v)
        signs = (1 - 2 * v, 2 * v - 1)
        for k in range(3):
            first, last = k + 1, 7 - k

            def dual_row(y, stores, k=k):
                for w, plan in enumerate((own, other)):
                    dual(k, w, y, plan[k][0], stores)
                if k == 0:
                    slopes(0, y, (-8, 0, 8), stores)
                    slopes(1, y, slope_other, stores)

            def body(y, carry, k=k, dual_row=dual_row, last=last):
                stores = []
                for w, plan in enumerate((own, other)):
                    primal(k, w, y, signs[w], plan[k][1], stores)
                dual_row(jnp.minimum(y + 1, last - 1), stores)
                flush(stores)
                return carry

            for y in (first - 1, first):
                stores = []
                dual_row(y, stores)
                flush(stores)
            lax.fori_loop(first, last, body, 0)
        stores = []
        slopes(0, 7, (-8, 0, 8), stores)
        slopes(1, 7, slope_other, stores)
        flush(stores)

    by_view(run)


def outer_kernel(sizes, m1_ref, m2_ref, g1_ref, g2_ref, *refs):
    refine_ref, dual_ref = refs[18:20]
    state = refs[20:38]
    MX, CV, XG, OUT = refs[38:]
    F, LO, HI = state[:3]
    XB, YB = state[16:]
    dual, primal, slopes = make_steps(sizes, state, MX, CV, XG, OUT)
    even_row = (lax.axis_index("row") & 1) == 0

    def above_below(at):
        one, two = g1_ref[at], g2_ref[at]
        return jnp.where(even_row, two, one), jnp.where(even_row, one, two)

    def run(v):
        own, own_narrow, other, other_narrow, slope_wide, slope_narrow = plans(v)
        signs = (1 - 2 * v, 2 * v - 1)
        for at, (plane, d, g) in enumerate(halo_slabs(v)):
            above, below = above_below(at)
            F[plane, 4 - d, SHIFT + g : SHIFT + g + 8] = above
            F[plane, 11 + d, SHIFT + g : SHIFT + g + 8] = below
        thin = SHIFT - 9 if v == 0 else SHIFT + 16
        for w in range(2):
            above, below = above_below(STRIP - 2 + w)
            spread_bounds(LO, HI, w, 0, above)
            spread_bounds(LO, HI, w, 2, below)
            if w == 0:
                for plane in (2, 3):
                    F[plane, 3, thin : thin + 1] = above[4 + plane : 5 + plane]
                    F[plane, 12, thin : thin + 1] = below[4 + plane : 5 + plane]
        stores = []
        for y in (-2, -1, 8, 9):
            slopes(0, y, (-5, 3, 5), stores)
        for y in (-1, 8):
            slopes(1, y, slope_wide, stores)
        for y in (-3, -2, 9, 10):
            slopes(1, y, slope_narrow, stores)
        flush(stores)

        def pairs(step):
            def body(i, carry):
                stores = []
                step(i, stores)
                flush(stores)
                return carry

            lax.fori_loop(0, 2, body, 0)

        def block(step):
            stores = []
            step(stores)
            flush(stores)

        for k in range(3):
            narrow_own = own_narrow if k < 2 else own[2]
            narrow_other = other_narrow if k == 0 else other[k]
            top_o, low_o = k - 4, 9 - k
            top_n, low_n = k - 3, 8 - k

            def dual_loop(i, stores):
                for y in (top_o + i, low_o + i):
                    dual(k, 0, y, narrow_own[0], stores)
                for y in (top_n + i, low_n + i):
                    dual(k, 1, y, narrow_other[0], stores)

            def dual_block(stores):
                for y in (k - 2, k - 1, 7 - k, 8 - k):
                    dual(k, 0, y, own[k][0], stores)
                for y in (k - 1, 7 - k):
                    dual(k, 1, y, other[k][0], stores)

            def primal_loop(i, stores):
                for y in (k - 3 + i, 9 - k + i):
                    primal(k, 0, y, signs[0], narrow_own[1], stores)
                for y in (k - 2 + i, 8 - k + i):
                    primal(k, 1, y, signs[1], narrow_other[1], stores)

            def primal_block(stores):
                for y in (k - 1, k, 7 - k, 8 - k):
                    primal(k, 0, y, signs[0], own[k][1], stores)
                for y in (k, 7 - k):
                    primal(k, 1, y, signs[1], other[k][1], stores)

            pairs(dual_loop)
            block(dual_block)
            pairs(primal_loop)
            block(primal_block)

        def last_dual(i, carry):
            stores = []
            for y in (3 * i - 1, 3 * i, 3 * i + 1):
                dual(3, 0, y, own[3][0], stores)
            flush(stores)
            return carry

        def last_primal(i, carry):
            stores = []
            for y in (4 * i, 4 * i + 1, 4 * i + 2, 4 * i + 3):
                primal(3, 0, y, signs[0], own[3][1], stores)
            flush(stores)
            return carry

        lax.fori_loop(0, 3, last_dual, 0)
        lax.fori_loop(0, 2, last_primal, 0)

    by_view(run)

    def from_slabs(slabs, put):
        parts = jnp.transpose(slabs, (1, 0, 2))
        for j in range(BLOCKS):
            put(slice(LANES * j, LANES * (j + 1)), parts[j])

    def put_refine(at, value):
        refine_ref[0, :, at] = value

    def put_x(at, value):
        dual_ref[0, 0, :, at] = value

    def put_y(at, value):
        dual_ref[0, 1, :, at] = value

    from_slabs(OUT[...], put_refine)
    from_slabs(XB[0, 4:12, SHIFT : SHIFT + 8], put_x)
    from_slabs(YB[0, 4:12, SHIFT : SHIFT + 8], put_y)


def on_device(sizes, image, coarse, bounds):
    f32 = jnp.float32
    vmem = pl.BlockSpec(memory_space=pltpu.VMEM)
    hbm = pl.BlockSpec(memory_space=pltpu.HBM)
    params = pltpu.CompilerParams(vmem_limit_bytes=VMEM_BYTES)
    own, edge = pl.pallas_call(
        pack_kernel,
        out_shape=(
            jax.ShapeDtypeStruct((TILE_PACK, BLOCKS, LANES), f32),
            jax.ShapeDtypeStruct((2, BLOCKS, LANES), f32),
        ),
        in_specs=[hbm] * 3,
        out_specs=(vmem,) * 2,
        scratch_shapes=[
            pltpu.VMEM(image.shape, f32),
            pltpu.VMEM(coarse.shape, jnp.int32),
            pltpu.SMEM(bounds.shape, jnp.int32),
            pltpu.SemaphoreType.DMA((3,)),
        ],
    )(image, coarse, bounds)
    other = swapped(own, lambda v, r, c: (1 - v, r, c), sizes)
    edge_own = swapped(edge, lambda v, r, c: (v, r, c ^ 1), sizes)
    edge_other = swapped(edge, lambda v, r, c: (1 - v, r, c ^ 1), sizes)
    both, more = pl.pallas_call(
        join_kernel,
        out_shape=(
            jax.ShapeDtypeStruct((2 * TILE_PACK, BLOCKS, LANES), f32),
            jax.ShapeDtypeStruct((2 * TILE_PACK + 3, BLOCKS, LANES), f32),
        ),
        in_specs=[vmem] * 4,
        out_specs=(vmem, vmem),
        compiler_params=params,
    )(own, other, edge_own, edge_other)
    side_b = swapped(more, lambda v, r, c: (v, r, ((c + 1) ^ 1) - 1), sizes)
    side_a = swapped(both, lambda v, r, c: (v, r, c ^ 1), sizes)
    near = pl.pallas_call(
        near_kernel,
        out_shape=jax.ShapeDtypeStruct((3, BLOCKS, LANES), f32),
        in_specs=[vmem],
        out_specs=vmem,
        compiler_params=params,
    )(side_b)
    far = swapped(near, lambda v, r, c: (v, r, c ^ 1), sizes)
    strip = jax.ShapeDtypeStruct((STRIP, 8, LANES), f32)

    def field(n, dtype=f32):
        return jax.ShapeDtypeStruct((n, TALL, WIDE, LANES), dtype)

    limits = jax.ShapeDtypeStruct((2, 3, WIDE, LANES), f32)
    m1, m2, *state = pl.pallas_call(
        assemble_kernel,
        out_shape=(strip, strip, field(4), limits, limits),
        in_specs=[vmem] * 4,
        out_specs=(vmem,) * 5,
        compiler_params=params,
    )(both, side_a, side_b, far)
    g2 = swapped(m2, lambda v, r, c: (v, ((r + 1) ^ 1) - 1, c), sizes)
    g1 = swapped(m1, lambda v, r, c: (v, r ^ 1, c), sizes)
    tables = [pltpu.VMEM((WIDE, LANES), f32), pltpu.VMEM((WIDE, LANES), f32), pltpu.VMEM((WIDE, LANES), jnp.int32)]
    fields = [field(2), field(2, jnp.int32)] + [field(2)] * 13
    more_state = pl.pallas_call(
        lambda *refs: inner_kernel(sizes, *refs),
        out_shape=tuple(fields),
        in_specs=[vmem] * 3,
        out_specs=(vmem,) * 15,
        scratch_shapes=tables,
        compiler_params=params,
        cost_estimate=pl.CostEstimate(flops=20_000_000, bytes_accessed=4_000_000, transcendentals=0),
    )(*state)
    state = [*state, *more_state]
    refine, dual, *_ = pl.pallas_call(
        lambda *refs: outer_kernel(sizes, *refs),
        out_shape=(
            jax.ShapeDtypeStruct((1, OUT_ROWS, BLOCKS * LANES), f32),
            jax.ShapeDtypeStruct((1, 2, OUT_ROWS, BLOCKS * LANES), f32),
            field(4),
            limits,
            limits,
            *fields,
        ),
        in_specs=[vmem] * 22,
        out_specs=(vmem,) * 20,
        input_output_aliases={4 + n: 2 + n for n in range(18)},
        scratch_shapes=[*tables, pltpu.VMEM((OUT_ROWS, BLOCKS, LANES), f32)],
        compiler_params=params,
    )(m1, m2, g1, g2, *state)
    return refine, dual


def solution(mesh):
    sizes = tuple(mesh.shape[axis] for axis in AXES)
    return jax.shard_map(
        lambda *args: on_device(sizes, *args),
        mesh=mesh,
        in_specs=(P("view", "row", "col"), P("view", "row", "col"), P("view", "row", "col", None)),
        out_specs=(P("view", "row", "col"), P("view", None, "row", "col")),
        check_vma=False,
    )
```

```python
import jax
import jax.numpy as jnp
from jax import lax
from jax.experimental import pallas as pl
from jax.experimental.pallas import tpu as pltpu
from jax.sharding import PartitionSpec as P

AXES = ("view", "row", "col")
LANES = 128
OUT_ROWS = 8
BLOCKS = 8
TILE_PACK = 17
STRIP = 36
SHIFT = 16
WIDE = 40
TALL = 16
VMEM_BYTES = 40 * 1024 * 1024

tau = 0.25
sigma = 0.5
huber_eps = 0.05
edge_gain = 2.0
slope_floor = 0.05
couple_weight = 0.5
data_weight = 1.0


def swapped(block, partner, sizes):
    views, rows, cols = sizes
    route = []
    for v in range(views):
        for r in range(rows):
            for c in range(cols):
                to_v, to_r, to_c = partner(v, r, c)
                if 0 <= to_r < rows and 0 <= to_c < cols:
                    route.append(((v * rows + r) * cols + c, (to_v * rows + to_r) * cols + to_c))
    return lax.ppermute(block, AXES, route)


def to_slabs(tile):
    parts = jnp.stack([tile[:, LANES * j : LANES * (j + 1)] for j in range(BLOCKS)])
    return jnp.transpose(parts, (1, 0, 2))


def pack_kernel(image_hbm, coarse_hbm, bounds_hbm, out_ref, edge_ref, image_ref, coarse_ref, bounds_ref, sems):
    copies = [
        pltpu.make_async_copy(source, target, sems.at[n])
        for n, (source, target) in enumerate(
            ((image_hbm, image_ref), (coarse_hbm, coarse_ref), (bounds_hbm, bounds_ref))
        )
    ]
    for copy in copies:
        copy.start()
    odd = (lax.axis_index("col") & 1) == 1
    last = (BLOCKS - 1) * LANES
    copies[0].wait()
    image = image_ref[0]
    out_ref[0:8] = to_slabs(image)
    edge_ref[0] = jnp.where(odd, image[:, :LANES], image[:, last:])
    copies[1].wait()
    coarse = coarse_ref[0].astype(jnp.float32)
    out_ref[8:16] = to_slabs(coarse)
    edge_ref[1] = jnp.where(odd, coarse[:, :LANES], coarse[:, last:])
    copies[2].wait()
    sub = lax.broadcasted_iota(jnp.int32, (BLOCKS, LANES), 0)
    out_ref[16] = jnp.where(sub == 0, bounds_ref[0, 0, 0, 0], bounds_ref[0, 0, 0, 1]).astype(jnp.float32)


def place_kernel(image_ref, coarse_ref, bounds_ref, out_ref):
    out_ref[0:8] = to_slabs(image_ref[0])
    out_ref[8:16] = to_slabs(coarse_ref[0].astype(jnp.float32))
    limits = bounds_ref[...].astype(jnp.float32)
    sub = lax.broadcasted_iota(jnp.int32, (BLOCKS, LANES), 0)
    low, high = (jnp.broadcast_to(limits[:, n : n + 1], (BLOCKS, LANES)) for n in range(2))
    out_ref[16] = jnp.where(sub == 0, low, high)


def join_kernel(own_ref, other_ref, edge_own_ref, edge_other_ref, both_ref, more_ref):
    for ref in (both_ref, more_ref):
        ref[0:TILE_PACK] = own_ref[...]
        ref[TILE_PACK : 2 * TILE_PACK] = other_ref[...]
    more_ref[2 * TILE_PACK] = edge_own_ref[0]
    more_ref[2 * TILE_PACK + 1 :] = edge_other_ref[...]


def near_kernel(b_ref, out_ref):
    odd = (lax.axis_index("col") & 1) == 1
    for n, base in enumerate((0, TILE_PACK, TILE_PACK + 8)):
        for y in range(8):
            out_ref[n, y : y + 1, :] = jnp.where(odd, b_ref[base + y, 0:1], b_ref[base + y, 7:8])


def halo_slabs(view):
    mid = (-5, 1) if view == 0 else (-1, 5)
    slabs = [(p, d, g) for p in (0, 1) for d in (1, 2) for g in (-8, 0, 8)]
    slabs += [(p, d, g) for p in (0, 1) for d in (3, 4) for g in (-1, 1)]
    slabs += [(p, 1, g) for p in (2, 3) for g in (-8, 0, 8)]
    slabs += [(p, d, g) for p in (2, 3) for d in (2, 3) for g in mid]
    return slabs


def assemble_kernel(both_ref, a_ref, b_ref, far_ref, m1_ref, m2_ref, F, LO, HI):
    odd = (lax.axis_index("col") & 1) == 1
    even_row = (lax.axis_index("row") & 1) == 0
    first = lax.axis_index("view") == 0
    zero = jnp.zeros((8, LANES), jnp.float32)
    m2_ref[STRIP] = zero
    for plane in range(4):
        base = (plane // 2) * TILE_PACK + (plane % 2) * 8
        for y in range(8):
            at = base + y
            F[plane, y + 4, 0:8] = zero
            F[plane, y + 4, 8:16] = jnp.where(odd, a_ref[at], b_ref[at])
            F[plane, y + 4, 16:24] = both_ref[at]
            F[plane, y + 4, 24:32] = jnp.where(odd, b_ref[at], a_ref[at])
            F[plane, y + 4, 32:40] = zero
    far, near = far_ref[...], b_ref[2 * TILE_PACK :]
    left, right = jnp.where(odd, far, near), jnp.where(odd, near, far)
    cross = jnp.where(first, left, right)
    low, high = SHIFT - 9, SHIFT + 16
    for y in range(8):
        row = slice(y, y + 1)
        F[0, y + 4, low : low + 1] = left[0, row]
        F[0, y + 4, high : high + 1] = right[0, row]
        for plane in (2, 3):
            F[plane, y + 4, low : low + 1] = cross[plane - 1, row]
            F[plane, y + 4, high : high + 1] = cross[plane - 1, row]

    def put(at, top, bottom):
        m1_ref[at] = jnp.where(even_row, bottom, top)
        m2_ref[at] = jnp.where(even_row, top, bottom)

    for at, ((plane, d, g), (_, _, g1)) in enumerate(zip(halo_slabs(0), halo_slabs(1), strict=True)):
        pair = []
        for ry in (3 + d, 12 - d):
            value = F[plane, ry, SHIFT + g : SHIFT + g + 8]
            if g1 != g:
                value = jnp.where(first, value, F[plane, ry, SHIFT + g1 : SHIFT + g1 + 8])
            pair.append(value)
        put(at, *pair)
    for w in range(2):
        s = w * TILE_PACK + 16
        tiles = (jnp.where(odd, a_ref[s], b_ref[s]), both_ref[s], jnp.where(odd, b_ref[s], a_ref[s]))
        thin = [jnp.concatenate([cross[1, y : y + 1], cross[2, y : y + 1]], axis=0) for y in (0, 7)]
        ends = [jnp.concatenate([t[0:2] for t in tiles] + [t], axis=0) for t in thin]
        put(STRIP - 2 + w, *ends)
        spread_bounds(LO, HI, w, 1, ends[0])


def spread_bounds(LO, HI, w, rg, rows):
    zero = jnp.zeros((8, LANES), jnp.float32)
    for j in range(3):
        at = SHIFT - 8 + 8 * j
        LO[w, rg, at : at + 8] = jnp.broadcast_to(rows[2 * j : 2 * j + 1], (8, LANES))
        HI[w, rg, at : at + 8] = jnp.broadcast_to(rows[2 * j + 1 : 2 * j + 2], (8, LANES))
    for ref in (LO, HI):
        ref[w, rg, 0:8] = zero
        ref[w, rg, 32:40] = zero


def plans(view):
    if view == 0:
        other_wide = (((-9, -1, 4), (-8, 0, 4)), ((-5, 1), (-5, 1)), ((-5, 0), (-4, 0)))
        other_narrow = ((-5, 1), (-5, 1))
        slope_wide, slope_narrow = (-9, -1, 5), (-5, 1)
    else:
        other_wide = (((-5, 3, 8), (-4, 4, 8)), ((-1, 5), (-1, 5)), ((-1, 4), (0, 4)))
        other_narrow = ((-1, 5), (-1, 5))
        slope_wide, slope_narrow = (-5, 3, 9), (-1, 5)
    own_wide = (((-5, 3, 5), (-5, 3, 5)), ((-5, 3, 4), (-4, 4)), ((-1, 1), (-1, 1)), ((-1, 0), (0,)))
    own_narrow = ((-1, 1), (-1, 1))
    return own_wide, own_narrow, other_wide, other_narrow, slope_wide, slope_narrow


def make_steps(sizes, state, MX, CV, XG, OUT):
    (F, LO, HI, G, D, RES, SL, INV, RD, IE, UA, RA, UB, RB, XA, YA, XB, YB) = state
    _, n_row, n_col = sizes
    view, row, col = lax.axis_index("view"), lax.axis_index("row"), lax.axis_index("col")
    lane = lax.broadcasted_iota(jnp.int32, (8, LANES), 1)
    sub = lax.broadcasted_iota(jnp.int32, (8, LANES), 0)
    total = n_col * BLOCKS * LANES
    u_bufs = (F, UA, UB, UA, None)
    ubar_bufs = (F, RA, RB, RA, None)
    p_bufs = (None, (XA, YA), (XB, YB), (XA, YA), (XB, YB))
    for i in range(0, WIDE, 8):
        x = (col * BLOCKS + (i - SHIFT) + sub) * LANES
        XG[i : i + 8] = x
        valid = (x >= 0) & (x < total)
        CV[i : i + 8] = jnp.where(valid, 1.0, 0.0)
        MX[i : i + 8] = jnp.where(valid & (x + lane < total - 1), 1.0, 0.0)

    def ahead(ref, lead, i):
        here, after = ref[(*lead, pl.ds(i, 8))], ref[(*lead, pl.ds(i + 1, 8))]
        return here, pltpu.roll(jnp.where(lane == 0, after, here), LANES - 1, 1)

    def behind(ref, lead, i):
        here, before = ref[(*lead, pl.ds(i, 8))], ref[(*lead, pl.ds(i - 1, 8))]
        return here, pltpu.roll(jnp.where(lane == LANES - 1, before, here), 1, 1)

    def masks(ry):
        y = row * OUT_ROWS + ry - 4
        ok = jnp.where((y >= 0) & (y < n_row * OUT_ROWS), 1.0, 0.0)
        down = jnp.where((y >= 0) & (y < n_row * OUT_ROWS - 1), 1.0, 0.0)
        return ok, down

    def dual_step(k, w, ry, starts, ubar, p_in, p_out, stores):
        ok, down = masks(ry)
        for g in starts:
            i = g + SHIFT
            mx = MX[i : i + 8] * ok
            my = CV[i : i + 8] * down
            here_at = (w, ry, pl.ds(i, 8))
            if k == 0:
                here, right = ahead(F, (2 * w, ry), i)
                gx, gy = (right - here) * mx, (F[2 * w, ry + 1, pl.ds(i, 8)] - here) * my
                inverse = 1.0 + edge_gain * (gx * gx + gy * gy)
                ie = inverse * inverse
                stores.append((IE, here_at, ie))
            else:
                ie = IE[here_at]
            lead = (2 * w + 1, ry) if k == 0 else (w, ry)
            lead_down = (2 * w + 1, ry + 1) if k == 0 else (w, ry + 1)
            here, right = ahead(ubar, lead, i)
            gx = (right - here) * mx
            gy = (ubar[(*lead_down, pl.ds(i, 8))] - here) * my
            if k == 0:
                qx, qy = sigma * gx, sigma * gy
            else:
                qx = p_in[0][here_at] + sigma * gx
                qy = p_in[1][here_at] + sigma * gy
            qx, qy = qx * (1.0 / (1.0 + sigma * huber_eps)), qy * (1.0 / (1.0 + sigma * huber_eps))
            shrink = lax.rsqrt(jnp.maximum(1.0, (qx * qx + qy * qy) * ie))
            stores.append((p_out[0], here_at, qx * shrink))
            stores.append((p_out[1], here_at, qy * shrink))

    def primal_step(k, w, sign, ry, starts, u_in, p_out, u_out, ubar_out, stores):
        ok, _ = masks(ry)
        rg = sum(int(ry >= n) if isinstance(ry, int) else (ry >= n).astype(jnp.int32) for n in (4, 12))
        for g in starts:
            i = g + SHIFT
            here = pl.ds(i, 8)
            here_at = (w, ry, here)
            d0 = F[2 * w + 1, ry, here]
            if k == 0:
                t = lane - sign * d0.astype(jnp.int32)
                stores.append((D, here_at, t))
            else:
                t = D[here_at]
            place, hop = t & (LANES - 1), t >> 7
            picks = [hop == -sign * m for m in range(1, 5)]

            def read(ref, lead):
                value = jnp.take_along_axis(ref[(*lead, here)], place, axis=1)
                for m in range(1, 5):
                    more = jnp.take_along_axis(ref[(*lead, pl.ds(i - sign * m, 8))], place, axis=1)
                    value = jnp.where(picks[m - 1], more, value)
                return value

            if k == 0:
                residue = read(F, (2 * (1 - w), ry)) - F[2 * w, ry, here]
                slope = read(G, (1 - w, ry)) * float(-sign)
                inv = 1.0 / jnp.maximum(slope * slope, slope_floor)
                target = XG[i : i + 8] + t
                inside = (target >= 0) & (target < total)
                rden = jnp.where(inside, 1.0 / (1.0 + tau * couple_weight), 1.0)
                stores += [(RES, here_at, residue), (SL, here_at, slope), (INV, here_at, inv), (RD, here_at, rden)]
            else:
                residue, slope = RES[here_at], SL[here_at]
                inv, rden = INV[here_at], RD[here_at]
            partner = read(u_in, (2 * (1 - w) + 1, ry) if k == 0 else (1 - w, ry))
            u = d0 if k == 0 else u_in[here_at]
            px, px_left = behind(p_out[0], (w, ry), i)
            div = px - px_left + p_out[1][here_at] - p_out[1][w, ry - 1, here]
            blended = (u + tau * div + (tau * couple_weight) * partner) * rden
            mismatch = residue + slope * (blended - d0)
            limit = (data_weight * tau) * rden
            step = jnp.minimum(jnp.maximum(mismatch * inv, -limit), limit)
            new = jnp.minimum(jnp.maximum(blended - slope * step, LO[w, rg, here]), HI[w, rg, here])
            if k < 3:
                new = new * (CV[i : i + 8] * ok)
                stores.append((u_out, here_at, new))
                stores.append((ubar_out, here_at, 2.0 * new - u))
            else:
                stores.append((OUT, (ry - 4,), new - d0))

    def slope_step(w, ry, starts, stores):
        for g in starts:
            i = g + SHIFT
            _, right = ahead(F, (2 * w, ry), i)
            _, left = behind(F, (2 * w, ry), i)
            stores.append((G, (w, ry, pl.ds(i, 8)), (right - left) * 0.5))

    def dual(k, w, y, starts, stores):
        dual_step(k, w, y + 4, starts, ubar_bufs[k], p_bufs[k], p_bufs[k + 1], stores)

    def primal(k, w, y, sign, starts, stores):
        primal_step(k, w, sign, y + 4, starts, u_bufs[k], p_bufs[k + 1], u_bufs[k + 1], ubar_bufs[k + 1], stores)

    def slopes(w, y, starts, stores):
        slope_step(w, y + 4, starts, stores)

    return dual, primal, slopes


def flush(stores):
    for ref, at, value in stores:
        ref[at] = value


def by_view(run):
    view = lax.axis_index("view")

    @pl.when(view == 0)
    def _():
        run(0)

    @pl.when(view == 1)
    def _():
        run(1)


def inner_kernel(sizes, F, LO, HI, *refs):
    state, (MX, CV, XG) = (F, LO, HI, *refs[:15]), refs[15:]
    dual, primal, slopes = make_steps(sizes, state, MX, CV, XG, None)

    def run(v):
        own, _, other, _, slope_other, _ = plans(v)
        signs = (1 - 2 * v, 2 * v - 1)
        for k in range(3):
            first, last = k + 1, 7 - k

            def dual_row(y, stores, k=k):
                for w, plan in enumerate((own, other)):
                    dual(k, w, y, plan[k][0], stores)
                if k == 0:
                    slopes(0, y, (-8, 0, 8), stores)
                    slopes(1, y, slope_other, stores)

            def body(y, carry, k=k, dual_row=dual_row, last=last):
                stores = []
                for w, plan in enumerate((own, other)):
                    primal(k, w, y, signs[w], plan[k][1], stores)
                dual_row(jnp.minimum(y + 1, last - 1), stores)
                flush(stores)
                return carry

            for y in (first - 1, first):
                stores = []
                dual_row(y, stores)
                flush(stores)
            lax.fori_loop(first, last, body, 0)
        stores = []
        slopes(0, 7, (-8, 0, 8), stores)
        slopes(1, 7, slope_other, stores)
        flush(stores)

    by_view(run)


def outer_kernel(sizes, m1_ref, m2_ref, g1_ref, g2_ref, *refs):
    refine_ref, dual_ref = refs[18:20]
    state = refs[20:38]
    MX, CV, XG, OUT = refs[38:]
    F, LO, HI = state[:3]
    XB, YB = state[16:]
    dual, primal, slopes = make_steps(sizes, state, MX, CV, XG, OUT)
    even_row = (lax.axis_index("row") & 1) == 0

    def above_below(at):
        one, two = g1_ref[at], g2_ref[at]
        return jnp.where(even_row, two, one), jnp.where(even_row, one, two)

    def run(v):
        own, own_narrow, other, other_narrow, slope_wide, slope_narrow = plans(v)
        signs = (1 - 2 * v, 2 * v - 1)
        for at, (plane, d, g) in enumerate(halo_slabs(v)):
            above, below = above_below(at)
            F[plane, 4 - d, SHIFT + g : SHIFT + g + 8] = above
            F[plane, 11 + d, SHIFT + g : SHIFT + g + 8] = below
        thin = SHIFT - 9 if v == 0 else SHIFT + 16
        for w in range(2):
            above, below = above_below(STRIP - 2 + w)
            spread_bounds(LO, HI, w, 0, above)
            spread_bounds(LO, HI, w, 2, below)
            if w == 0:
                for plane in (2, 3):
                    F[plane, 3, thin : thin + 1] = above[4 + plane : 5 + plane]
                    F[plane, 12, thin : thin + 1] = below[4 + plane : 5 + plane]
        stores = []
        for y in (-2, -1, 8, 9):
            slopes(0, y, (-5, 3, 5), stores)
        for y in (-1, 8):
            slopes(1, y, slope_wide, stores)
        for y in (-3, -2, 9, 10):
            slopes(1, y, slope_narrow, stores)
        flush(stores)

        def pairs(step):
            def body(i, carry):
                stores = []
                step(i, stores)
                flush(stores)
                return carry

            lax.fori_loop(0, 2, body, 0)

        def block(step):
            stores = []
            step(stores)
            flush(stores)

        for k in range(3):
            narrow_own = own_narrow if k < 2 else own[2]
            narrow_other = other_narrow if k == 0 else other[k]
            top_o, low_o = k - 4, 9 - k
            top_n, low_n = k - 3, 8 - k

            def dual_loop(i, stores):
                for y in (top_o + i, low_o + i):
                    dual(k, 0, y, narrow_own[0], stores)
                for y in (top_n + i, low_n + i):
                    dual(k, 1, y, narrow_other[0], stores)

            def dual_block(stores):
                for y in (k - 2, k - 1, 7 - k, 8 - k):
                    dual(k, 0, y, own[k][0], stores)
                for y in (k - 1, 7 - k):
                    dual(k, 1, y, other[k][0], stores)

            def primal_loop(i, stores):
                for y in (k - 3 + i, 9 - k + i):
                    primal(k, 0, y, signs[0], narrow_own[1], stores)
                for y in (k - 2 + i, 8 - k + i):
                    primal(k, 1, y, signs[1], narrow_other[1], stores)

            def primal_block(stores):
                for y in (k - 1, k, 7 - k, 8 - k):
                    primal(k, 0, y, signs[0], own[k][1], stores)
                for y in (k, 7 - k):
                    primal(k, 1, y, signs[1], other[k][1], stores)

            pairs(dual_loop)
            block(dual_block)
            pairs(primal_loop)
            block(primal_block)

        def last_dual(i, carry):
            stores = []
            for y in (3 * i - 1, 3 * i, 3 * i + 1):
                dual(3, 0, y, own[3][0], stores)
            flush(stores)
            return carry

        def last_primal(i, carry):
            stores = []
            for y in (4 * i, 4 * i + 1, 4 * i + 2, 4 * i + 3):
                primal(3, 0, y, signs[0], own[3][1], stores)
            flush(stores)
            return carry

        lax.fori_loop(0, 3, last_dual, 0)
        lax.fori_loop(0, 2, last_primal, 0)

    by_view(run)

    def from_slabs(slabs, put):
        parts = jnp.transpose(slabs, (1, 0, 2))
        for j in range(BLOCKS):
            put(slice(LANES * j, LANES * (j + 1)), parts[j])

    def put_refine(at, value):
        refine_ref[0, :, at] = value

    def put_x(at, value):
        dual_ref[0, 0, :, at] = value

    def put_y(at, value):
        dual_ref[0, 1, :, at] = value

    from_slabs(OUT[...], put_refine)
    from_slabs(XB[0, 4:12, SHIFT : SHIFT + 8], put_x)
    from_slabs(YB[0, 4:12, SHIFT : SHIFT + 8], put_y)


def on_device(sizes, image, coarse, bounds):
    f32 = jnp.float32
    vmem = pl.BlockSpec(memory_space=pltpu.VMEM)
    hbm = pl.BlockSpec(memory_space=pltpu.HBM)
    params = pltpu.CompilerParams(vmem_limit_bytes=VMEM_BYTES)
    own, edge = pl.pallas_call(
        pack_kernel,
        out_shape=(
            jax.ShapeDtypeStruct((TILE_PACK, BLOCKS, LANES), f32),
            jax.ShapeDtypeStruct((2, BLOCKS, LANES), f32),
        ),
        in_specs=[hbm] * 3,
        out_specs=(vmem,) * 2,
        scratch_shapes=[
            pltpu.VMEM(image.shape, f32),
            pltpu.VMEM(coarse.shape, jnp.int32),
            pltpu.SMEM(bounds.shape, jnp.int32),
            pltpu.SemaphoreType.DMA((3,)),
        ],
    )(image, coarse, bounds)
    other = swapped(own, lambda v, r, c: (1 - v, r, c), sizes)
    edge_own = swapped(edge, lambda v, r, c: (v, r, c ^ 1), sizes)
    edge_other = swapped(edge, lambda v, r, c: (1 - v, r, c ^ 1), sizes)
    placed = pl.pallas_call(
        place_kernel,
        out_shape=jax.ShapeDtypeStruct((TILE_PACK, BLOCKS, LANES), f32),
        in_specs=[vmem] * 3,
        out_specs=vmem,
        compiler_params=params,
        cost_estimate=pl.CostEstimate(flops=4_000_000, bytes_accessed=200_000, transcendentals=0),
    )(image, coarse, bounds.reshape(1, 2))
    both, more = pl.pallas_call(
        join_kernel,
        out_shape=(
            jax.ShapeDtypeStruct((2 * TILE_PACK, BLOCKS, LANES), f32),
            jax.ShapeDtypeStruct((2 * TILE_PACK + 3, BLOCKS, LANES), f32),
        ),
        in_specs=[vmem] * 4,
        out_specs=(vmem, vmem),
        compiler_params=params,
    )(placed, other, edge_own, edge_other)
    side_b = swapped(more, lambda v, r, c: (v, r, ((c + 1) ^ 1) - 1), sizes)
    side_a = swapped(both, lambda v, r, c: (v, r, c ^ 1), sizes)
    near = pl.pallas_call(
        near_kernel,
        out_shape=jax.ShapeDtypeStruct((3, BLOCKS, LANES), f32),
        in_specs=[vmem],
        out_specs=vmem,
        compiler_params=params,
    )(side_b)
    far = swapped(near, lambda v, r, c: (v, r, c ^ 1), sizes)
    strip = jax.ShapeDtypeStruct((STRIP, 8, LANES), f32)
    longer = jax.ShapeDtypeStruct((STRIP + 1, 8, LANES), f32)

    def field(n, dtype=f32):
        return jax.ShapeDtypeStruct((n, TALL, WIDE, LANES), dtype)

    limits = jax.ShapeDtypeStruct((2, 3, WIDE, LANES), f32)
    m1, m2, *state = pl.pallas_call(
        assemble_kernel,
        out_shape=(strip, longer, field(4), limits, limits),
        in_specs=[vmem] * 4,
        out_specs=(vmem,) * 5,
        compiler_params=params,
    )(both, side_a, side_b, far)
    g2 = swapped(m2, lambda v, r, c: (v, ((r + 1) ^ 1) - 1, c), sizes)
    g1 = swapped(m1, lambda v, r, c: (v, r ^ 1, c), sizes)
    tables = [pltpu.VMEM((WIDE, LANES), f32), pltpu.VMEM((WIDE, LANES), f32), pltpu.VMEM((WIDE, LANES), jnp.int32)]
    fields = [field(2), field(2, jnp.int32)] + [field(2)] * 13
    more_state = pl.pallas_call(
        lambda *refs: inner_kernel(sizes, *refs),
        out_shape=tuple(fields),
        in_specs=[vmem] * 3,
        out_specs=(vmem,) * 15,
        scratch_shapes=tables,
        compiler_params=params,
        cost_estimate=pl.CostEstimate(flops=20_000_000, bytes_accessed=4_000_000, transcendentals=0),
    )(*state)
    state = [*state, *more_state]
    refine, dual, *_ = pl.pallas_call(
        lambda *refs: outer_kernel(sizes, *refs),
        out_shape=(
            jax.ShapeDtypeStruct((1, OUT_ROWS, BLOCKS * LANES), f32),
            jax.ShapeDtypeStruct((1, 2, OUT_ROWS, BLOCKS * LANES), f32),
            field(4),
            limits,
            limits,
            *fields,
        ),
        in_specs=[vmem] * 22,
        out_specs=(vmem,) * 20,
        input_output_aliases={4 + n: 2 + n for n in range(18)},
        scratch_shapes=[*tables, pltpu.VMEM((OUT_ROWS, BLOCKS, LANES), f32)],
        compiler_params=params,
    )(m1, m2, g1, g2, *state)
    return refine, dual


def solution(mesh):
    sizes = tuple(mesh.shape[axis] for axis in AXES)
    return jax.shard_map(
        lambda *args: on_device(sizes, *args),
        mesh=mesh,
        in_specs=(P("view", "row", "col"), P("view", "row", "col"), P("view", "row", "col", None)),
        out_specs=(P("view", "row", "col"), P("view", None, "row", "col")),
        check_vma=False,
    )
```

```python
import jax
import jax.numpy as jnp
from jax import lax
from jax.experimental import pallas as pl
from jax.experimental.pallas import tpu as pltpu
from jax.sharding import PartitionSpec as P

AXES = ("view", "row", "col")
LANES = 128
OUT_ROWS = 8
BLOCKS = 8
TILE_PACK = 17
STRIP = 36
SHIFT = 16
WIDE = 40
TALL = 16
VMEM_BYTES = 40 * 1024 * 1024

tau = 0.25
sigma = 0.5
huber_eps = 0.05
edge_gain = 2.0
slope_floor = 0.05
couple_weight = 0.5
data_weight = 1.0


def swapped(block, partner, sizes):
    views, rows, cols = sizes
    route = []
    for v in range(views):
        for r in range(rows):
            for c in range(cols):
                to_v, to_r, to_c = partner(v, r, c)
                if 0 <= to_r < rows and 0 <= to_c < cols:
                    route.append(((v * rows + r) * cols + c, (to_v * rows + to_r) * cols + to_c))
    return lax.ppermute(block, AXES, route)


def to_slabs(tile):
    parts = jnp.stack([tile[:, LANES * j : LANES * (j + 1)] for j in range(BLOCKS)])
    return jnp.transpose(parts, (1, 0, 2))


def pack_kernel(image_hbm, coarse_hbm, bounds_hbm, out_ref, longer_ref, image_ref, coarse_ref, bounds_ref, sems):
    copies = [
        pltpu.make_async_copy(source, target, sems.at[n])
        for n, (source, target) in enumerate(
            ((image_hbm, image_ref), (coarse_hbm, coarse_ref), (bounds_hbm, bounds_ref))
        )
    ]
    for copy in copies:
        copy.start()
    copies[0].wait()
    image = image_ref[0]
    slabs = to_slabs(image)
    out_ref[0:8] = slabs
    longer_ref[0:8] = slabs
    copies[1].wait()
    coarse = coarse_ref[0].astype(jnp.float32)
    slabs = to_slabs(coarse)
    out_ref[8:16] = slabs
    longer_ref[8:16] = slabs
    copies[2].wait()
    sub = lax.broadcasted_iota(jnp.int32, (BLOCKS, LANES), 0)
    limits = jnp.where(sub == 0, bounds_ref[0, 0, 0, 0], bounds_ref[0, 0, 0, 1]).astype(jnp.float32)
    out_ref[16] = limits
    longer_ref[16] = limits
    longer_ref[17] = jnp.zeros((BLOCKS, LANES), jnp.float32)


def place_kernel(own_ref, out_ref):
    out_ref[...] = own_ref[...]


def join_kernel(own_ref, other_ref, a_ref, more_ref):
    odd = (lax.axis_index("col") & 1) == 1
    more_ref[0:TILE_PACK] = own_ref[...]
    more_ref[TILE_PACK : 2 * TILE_PACK] = other_ref[0:TILE_PACK]
    for n in range(2):
        for y in range(8):
            at = 8 * n + y
            more_ref[2 * TILE_PACK + n, y : y + 1, :] = jnp.where(odd, a_ref[at, 7:8], a_ref[at, 0:1])


def near_kernel(b_ref, out_ref, thin_ref):
    odd = (lax.axis_index("col") & 1) == 1
    for n, base in enumerate((0, TILE_PACK, TILE_PACK + 8)):
        for y in range(8):
            out_ref[n, y : y + 1, :] = jnp.where(odd, b_ref[base + y, 0:1], b_ref[base + y, 7:8])
    for n in range(2):
        thin_ref[n] = b_ref[2 * TILE_PACK + n]


def halo_slabs(view):
    mid = (-5, 1) if view == 0 else (-1, 5)
    slabs = [(p, d, g) for p in (0, 1) for d in (1, 2) for g in (-8, 0, 8)]
    slabs += [(p, d, g) for p in (0, 1) for d in (3, 4) for g in (-1, 1)]
    slabs += [(p, 1, g) for p in (2, 3) for g in (-8, 0, 8)]
    slabs += [(p, d, g) for p in (2, 3) for d in (2, 3) for g in mid]
    return slabs


def assemble_kernel(both_ref, a_own_ref, a_other_ref, b_ref, far_ref, cross_ref, m1_ref, m2_ref, F, LO, HI):
    odd = (lax.axis_index("col") & 1) == 1
    even_row = (lax.axis_index("row") & 1) == 0
    first = lax.axis_index("view") == 0
    zero = jnp.zeros((8, LANES), jnp.float32)
    m2_ref[STRIP] = zero
    for plane in range(4):
        base = (plane // 2) * TILE_PACK + (plane % 2) * 8
        a_ref = (a_own_ref, a_other_ref)[plane // 2]
        for y in range(8):
            at, a_tile = base + y, a_ref[(plane % 2) * 8 + y]
            F[plane, y + 4, 0:8] = zero
            F[plane, y + 4, 8:16] = jnp.where(odd, a_tile, b_ref[at])
            F[plane, y + 4, 16:24] = both_ref[at]
            F[plane, y + 4, 24:32] = jnp.where(odd, b_ref[at], a_tile)
            F[plane, y + 4, 32:40] = zero
    far = far_ref[...]
    near = (b_ref[2 * TILE_PACK], cross_ref[0], cross_ref[1])
    left = [jnp.where(odd, far[n], near[n]) for n in range(3)]
    right = [jnp.where(odd, near[n], far[n]) for n in range(3)]
    cross = [jnp.where(first, one, two) for one, two in zip(left, right, strict=True)]
    low, high = SHIFT - 9, SHIFT + 16
    for y in range(8):
        row = slice(y, y + 1)
        F[0, y + 4, low : low + 1] = left[0][row]
        F[0, y + 4, high : high + 1] = right[0][row]
        for plane in (2, 3):
            F[plane, y + 4, low : low + 1] = cross[plane - 1][row]
            F[plane, y + 4, high : high + 1] = cross[plane - 1][row]

    def put(at, top, bottom):
        m1_ref[at] = jnp.where(even_row, bottom, top)
        m2_ref[at] = jnp.where(even_row, top, bottom)

    for at, ((plane, d, g), (_, _, g1)) in enumerate(zip(halo_slabs(0), halo_slabs(1), strict=True)):
        pair = []
        for ry in (3 + d, 12 - d):
            value = F[plane, ry, SHIFT + g : SHIFT + g + 8]
            if g1 != g:
                value = jnp.where(first, value, F[plane, ry, SHIFT + g1 : SHIFT + g1 + 8])
            pair.append(value)
        put(at, *pair)
    for w in range(2):
        s = w * TILE_PACK + 16
        a_tile = (a_own_ref, a_other_ref)[w][16]
        tiles = (jnp.where(odd, a_tile, b_ref[s]), both_ref[s], jnp.where(odd, b_ref[s], a_tile))
        thin = [jnp.concatenate([cross[1][y : y + 1], cross[2][y : y + 1]], axis=0) for y in (0, 7)]
        ends = [jnp.concatenate([t[0:2] for t in tiles] + [t], axis=0) for t in thin]
        put(STRIP - 2 + w, *ends)
        spread_bounds(LO, HI, w, 1, ends[0])


def spread_bounds(LO, HI, w, rg, rows):
    zero = jnp.zeros((8, LANES), jnp.float32)
    for j in range(3):
        at = SHIFT - 8 + 8 * j
        LO[w, rg, at : at + 8] = jnp.broadcast_to(rows[2 * j : 2 * j + 1], (8, LANES))
        HI[w, rg, at : at + 8] = jnp.broadcast_to(rows[2 * j + 1 : 2 * j + 2], (8, LANES))
    for ref in (LO, HI):
        ref[w, rg, 0:8] = zero
        ref[w, rg, 32:40] = zero


def plans(view):
    if view == 0:
        other_wide = (((-9, -1, 4), (-8, 0, 4)), ((-5, 1), (-5, 1)), ((-5, 0), (-4, 0)))
        other_narrow = ((-5, 1), (-5, 1))
        slope_wide, slope_narrow = (-9, -1, 5), (-5, 1)
    else:
        other_wide = (((-5, 3, 8), (-4, 4, 8)), ((-1, 5), (-1, 5)), ((-1, 4), (0, 4)))
        other_narrow = ((-1, 5), (-1, 5))
        slope_wide, slope_narrow = (-5, 3, 9), (-1, 5)
    own_wide = (((-5, 3, 5), (-5, 3, 5)), ((-5, 3, 4), (-4, 4)), ((-1, 1), (-1, 1)), ((-1, 0), (0,)))
    own_narrow = ((-1, 1), (-1, 1))
    return own_wide, own_narrow, other_wide, other_narrow, slope_wide, slope_narrow


def make_steps(sizes, state, MX, CV, XG, OUT):
    (F, LO, HI, G, D, RES, SL, INV, RD, IE, UA, RA, UB, RB, XA, YA, XB, YB) = state
    _, n_row, n_col = sizes
    view, row, col = lax.axis_index("view"), lax.axis_index("row"), lax.axis_index("col")
    lane = lax.broadcasted_iota(jnp.int32, (8, LANES), 1)
    sub = lax.broadcasted_iota(jnp.int32, (8, LANES), 0)
    total = n_col * BLOCKS * LANES
    u_bufs = (F, UA, UB, UA, None)
    ubar_bufs = (F, RA, RB, RA, None)
    p_bufs = (None, (XA, YA), (XB, YB), (XA, YA), (XB, YB))
    for i in range(0, WIDE, 8):
        x = (col * BLOCKS + (i - SHIFT) + sub) * LANES
        XG[i : i + 8] = x
        valid = (x >= 0) & (x < total)
        CV[i : i + 8] = jnp.where(valid, 1.0, 0.0)
        MX[i : i + 8] = jnp.where(valid & (x + lane < total - 1), 1.0, 0.0)

    def ahead(ref, lead, i):
        here, after = ref[(*lead, pl.ds(i, 8))], ref[(*lead, pl.ds(i + 1, 8))]
        return here, pltpu.roll(jnp.where(lane == 0, after, here), LANES - 1, 1)

    def behind(ref, lead, i):
        here, before = ref[(*lead, pl.ds(i, 8))], ref[(*lead, pl.ds(i - 1, 8))]
        return here, pltpu.roll(jnp.where(lane == LANES - 1, before, here), 1, 1)

    def masks(ry):
        y = row * OUT_ROWS + ry - 4
        ok = jnp.where((y >= 0) & (y < n_row * OUT_ROWS), 1.0, 0.0)
        down = jnp.where((y >= 0) & (y < n_row * OUT_ROWS - 1), 1.0, 0.0)
        return ok, down

    def dual_step(k, w, ry, starts, ubar, p_in, p_out, stores):
        ok, down = masks(ry)
        for g in starts:
            i = g + SHIFT
            mx = MX[i : i + 8] * ok
            my = CV[i : i + 8] * down
            here_at = (w, ry, pl.ds(i, 8))
            if k == 0:
                here, right = ahead(F, (2 * w, ry), i)
                gx, gy = (right - here) * mx, (F[2 * w, ry + 1, pl.ds(i, 8)] - here) * my
                inverse = 1.0 + edge_gain * (gx * gx + gy * gy)
                ie = inverse * inverse
                stores.append((IE, here_at, ie))
            else:
                ie = IE[here_at]
            lead = (2 * w + 1, ry) if k == 0 else (w, ry)
            lead_down = (2 * w + 1, ry + 1) if k == 0 else (w, ry + 1)
            here, right = ahead(ubar, lead, i)
            gx = (right - here) * mx
            gy = (ubar[(*lead_down, pl.ds(i, 8))] - here) * my
            if k == 0:
                qx, qy = sigma * gx, sigma * gy
            else:
                qx = p_in[0][here_at] + sigma * gx
                qy = p_in[1][here_at] + sigma * gy
            qx, qy = qx * (1.0 / (1.0 + sigma * huber_eps)), qy * (1.0 / (1.0 + sigma * huber_eps))
            shrink = lax.rsqrt(jnp.maximum(1.0, (qx * qx + qy * qy) * ie))
            stores.append((p_out[0], here_at, qx * shrink))
            stores.append((p_out[1], here_at, qy * shrink))

    def primal_step(k, w, sign, ry, starts, u_in, p_out, u_out, ubar_out, stores):
        ok, _ = masks(ry)
        rg = sum(int(ry >= n) if isinstance(ry, int) else (ry >= n).astype(jnp.int32) for n in (4, 12))
        for g in starts:
            i = g + SHIFT
            here = pl.ds(i, 8)
            here_at = (w, ry, here)
            d0 = F[2 * w + 1, ry, here]
            if k == 0:
                t = lane - sign * d0.astype(jnp.int32)
                stores.append((D, here_at, t))
            else:
                t = D[here_at]
            place, hop = t & (LANES - 1), t >> 7
            picks = [hop == -sign * m for m in range(1, 5)]

            def read(ref, lead):
                value = jnp.take_along_axis(ref[(*lead, here)], place, axis=1)
                for m in range(1, 5):
                    more = jnp.take_along_axis(ref[(*lead, pl.ds(i - sign * m, 8))], place, axis=1)
                    value = jnp.where(picks[m - 1], more, value)
                return value

            if k == 0:
                residue = read(F, (2 * (1 - w), ry)) - F[2 * w, ry, here]
                slope = read(G, (1 - w, ry)) * float(-sign)
                inv = 1.0 / jnp.maximum(slope * slope, slope_floor)
                target = XG[i : i + 8] + t
                inside = (target >= 0) & (target < total)
                rden = jnp.where(inside, 1.0 / (1.0 + tau * couple_weight), 1.0)
                stores += [(RES, here_at, residue), (SL, here_at, slope), (INV, here_at, inv), (RD, here_at, rden)]
            else:
                residue, slope = RES[here_at], SL[here_at]
                inv, rden = INV[here_at], RD[here_at]
            partner = read(u_in, (2 * (1 - w) + 1, ry) if k == 0 else (1 - w, ry))
            u = d0 if k == 0 else u_in[here_at]
            px, px_left = behind(p_out[0], (w, ry), i)
            div = px - px_left + p_out[1][here_at] - p_out[1][w, ry - 1, here]
            blended = (u + tau * div + (tau * couple_weight) * partner) * rden
            mismatch = residue + slope * (blended - d0)
            limit = (data_weight * tau) * rden
            step = jnp.minimum(jnp.maximum(mismatch * inv, -limit), limit)
            new = jnp.minimum(jnp.maximum(blended - slope * step, LO[w, rg, here]), HI[w, rg, here])
            if k < 3:
                new = new * (CV[i : i + 8] * ok)
                stores.append((u_out, here_at, new))
                stores.append((ubar_out, here_at, 2.0 * new - u))
            else:
                stores.append((OUT, (ry - 4,), new - d0))

    def slope_step(w, ry, starts, stores):
        for g in starts:
            i = g + SHIFT
            _, right = ahead(F, (2 * w, ry), i)
            _, left = behind(F, (2 * w, ry), i)
            stores.append((G, (w, ry, pl.ds(i, 8)), (right - left) * 0.5))

    def dual(k, w, y, starts, stores):
        dual_step(k, w, y + 4, starts, ubar_bufs[k], p_bufs[k], p_bufs[k + 1], stores)

    def primal(k, w, y, sign, starts, stores):
        primal_step(k, w, sign, y + 4, starts, u_bufs[k], p_bufs[k + 1], u_bufs[k + 1], ubar_bufs[k + 1], stores)

    def slopes(w, y, starts, stores):
        slope_step(w, y + 4, starts, stores)

    return dual, primal, slopes


def flush(stores):
    for ref, at, value in stores:
        ref[at] = value


def by_view(run):
    view = lax.axis_index("view")

    @pl.when(view == 0)
    def _():
        run(0)

    @pl.when(view == 1)
    def _():
        run(1)


def inner_kernel(sizes, F, LO, HI, *refs):
    state, (MX, CV, XG) = (F, LO, HI, *refs[:15]), refs[15:]
    dual, primal, slopes = make_steps(sizes, state, MX, CV, XG, None)

    def run(v):
        own, _, other, _, slope_other, _ = plans(v)
        signs = (1 - 2 * v, 2 * v - 1)
        for k in range(3):
            first, last = k + 1, 7 - k

            def dual_row(y, stores, k=k):
                for w, plan in enumerate((own, other)):
                    dual(k, w, y, plan[k][0], stores)
                if k == 0:
                    slopes(0, y, (-8, 0, 8), stores)
                    slopes(1, y, slope_other, stores)

            for y in (first - 1, first):
                stores = []
                dual_row(y, stores)
                flush(stores)
            for y in range(first, last):
                stores = []
                for w, plan in enumerate((own, other)):
                    primal(k, w, y, signs[w], plan[k][1], stores)
                if y + 1 < last:
                    dual_row(y + 1, stores)
                flush(stores)
        stores = []
        slopes(0, 7, (-8, 0, 8), stores)
        slopes(1, 7, slope_other, stores)
        flush(stores)

    by_view(run)


def outer_kernel(sizes, m1_ref, m2_ref, g1_ref, g2_ref, *refs):
    refine_ref, dual_ref = refs[18:20]
    state = refs[20:38]
    MX, CV, XG, OUT = refs[38:]
    F, LO, HI = state[:3]
    XB, YB = state[16:]
    dual, primal, slopes = make_steps(sizes, state, MX, CV, XG, OUT)
    even_row = (lax.axis_index("row") & 1) == 0

    def above_below(at):
        one, two = g1_ref[at], g2_ref[at]
        return jnp.where(even_row, two, one), jnp.where(even_row, one, two)

    def run(v):
        own, own_narrow, other, other_narrow, slope_wide, slope_narrow = plans(v)
        signs = (1 - 2 * v, 2 * v - 1)
        for at, (plane, d, g) in enumerate(halo_slabs(v)):
            above, below = above_below(at)
            F[plane, 4 - d, SHIFT + g : SHIFT + g + 8] = above
            F[plane, 11 + d, SHIFT + g : SHIFT + g + 8] = below
        thin = SHIFT - 9 if v == 0 else SHIFT + 16
        for w in range(2):
            above, below = above_below(STRIP - 2 + w)
            spread_bounds(LO, HI, w, 0, above)
            spread_bounds(LO, HI, w, 2, below)
            if w == 0:
                for plane in (2, 3):
                    F[plane, 3, thin : thin + 1] = above[4 + plane : 5 + plane]
                    F[plane, 12, thin : thin + 1] = below[4 + plane : 5 + plane]
        stores = []
        for y in (-2, -1, 8, 9):
            slopes(0, y, (-5, 3, 5), stores)
        for y in (-1, 8):
            slopes(1, y, slope_wide, stores)
        for y in (-3, -2, 9, 10):
            slopes(1, y, slope_narrow, stores)
        flush(stores)

        def pairs(step):
            for i in range(2):
                stores = []
                step(i, stores)
                flush(stores)

        def block(step):
            stores = []
            step(stores)
            flush(stores)

        for k in range(3):
            narrow_own = own_narrow if k < 2 else own[2]
            narrow_other = other_narrow if k == 0 else other[k]
            top_o, low_o = k - 4, 9 - k
            top_n, low_n = k - 3, 8 - k

            def dual_loop(i, stores):
                for y in (top_o + i, low_o + i):
                    dual(k, 0, y, narrow_own[0], stores)
                for y in (top_n + i, low_n + i):
                    dual(k, 1, y, narrow_other[0], stores)

            def dual_block(stores):
                for y in (k - 2, k - 1, 7 - k, 8 - k):
                    dual(k, 0, y, own[k][0], stores)
                for y in (k - 1, 7 - k):
                    dual(k, 1, y, other[k][0], stores)

            def primal_loop(i, stores):
                for y in (k - 3 + i, 9 - k + i):
                    primal(k, 0, y, signs[0], narrow_own[1], stores)
                for y in (k - 2 + i, 8 - k + i):
                    primal(k, 1, y, signs[1], narrow_other[1], stores)

            def primal_block(stores):
                for y in (k - 1, k, 7 - k, 8 - k):
                    primal(k, 0, y, signs[0], own[k][1], stores)
                for y in (k, 7 - k):
                    primal(k, 1, y, signs[1], other[k][1], stores)

            pairs(dual_loop)
            block(dual_block)
            pairs(primal_loop)
            block(primal_block)

        def last_dual(i, stores):
            for y in (3 * i - 1, 3 * i, 3 * i + 1):
                dual(3, 0, y, own[3][0], stores)

        def last_primal(i, stores):
            for y in (4 * i, 4 * i + 1, 4 * i + 2, 4 * i + 3):
                primal(3, 0, y, signs[0], own[3][1], stores)

        for step, count in ((last_dual, 3), (last_primal, 2)):
            for i in range(count):
                stores = []
                step(i, stores)
                flush(stores)

    by_view(run)

    def from_slabs(slabs, put):
        parts = jnp.transpose(slabs, (1, 0, 2))
        for j in range(BLOCKS):
            put(slice(LANES * j, LANES * (j + 1)), parts[j])

    def put_refine(at, value):
        refine_ref[0, :, at] = value

    def put_x(at, value):
        dual_ref[0, 0, :, at] = value

    def put_y(at, value):
        dual_ref[0, 1, :, at] = value

    from_slabs(OUT[...], put_refine)
    from_slabs(XB[0, 4:12, SHIFT : SHIFT + 8], put_x)
    from_slabs(YB[0, 4:12, SHIFT : SHIFT + 8], put_y)


def on_device(sizes, image, coarse, bounds):
    f32 = jnp.float32
    vmem = pl.BlockSpec(memory_space=pltpu.VMEM)
    hbm = pl.BlockSpec(memory_space=pltpu.HBM)
    params = pltpu.CompilerParams(vmem_limit_bytes=VMEM_BYTES)
    tile = jax.ShapeDtypeStruct((TILE_PACK, BLOCKS, LANES), f32)
    own, longer = pl.pallas_call(
        pack_kernel,
        out_shape=(tile, jax.ShapeDtypeStruct((TILE_PACK + 1, BLOCKS, LANES), f32)),
        in_specs=[hbm] * 3,
        out_specs=(vmem, vmem),
        scratch_shapes=[
            pltpu.VMEM(image.shape, f32),
            pltpu.VMEM(coarse.shape, jnp.int32),
            pltpu.SMEM(bounds.shape, jnp.int32),
            pltpu.SemaphoreType.DMA((3,)),
        ],
    )(image, coarse, bounds)

    def in_pair(v, r, c):
        return v, r, c ^ 1

    def across(v, r, c):
        return 1 - v, r, c

    other = swapped(longer, across, sizes)
    a_own = swapped(own, in_pair, sizes)
    placed = pl.pallas_call(
        place_kernel,
        out_shape=tile,
        in_specs=[vmem],
        out_specs=vmem,
        compiler_params=params,
        cost_estimate=pl.CostEstimate(flops=4_000_000, bytes_accessed=200_000, transcendentals=0),
    )(own)
    more = pl.pallas_call(
        join_kernel,
        out_shape=jax.ShapeDtypeStruct((2 * TILE_PACK + 2, BLOCKS, LANES), f32),
        in_specs=[vmem] * 3,
        out_specs=vmem,
        compiler_params=params,
    )(placed, other, a_own)
    side_b = swapped(more, lambda v, r, c: (v, r, ((c + 1) ^ 1) - 1), sizes)
    a_other = swapped(other, in_pair, sizes)
    near, thin = pl.pallas_call(
        near_kernel,
        out_shape=(
            jax.ShapeDtypeStruct((3, BLOCKS, LANES), f32),
            jax.ShapeDtypeStruct((2, BLOCKS, LANES), f32),
        ),
        in_specs=[vmem],
        out_specs=(vmem, vmem),
        compiler_params=params,
    )(side_b)
    cross = swapped(thin, across, sizes)
    far = swapped(near, in_pair, sizes)
    strip = jax.ShapeDtypeStruct((STRIP, 8, LANES), f32)
    strip_longer = jax.ShapeDtypeStruct((STRIP + 1, 8, LANES), f32)

    def field(n, dtype=f32):
        return jax.ShapeDtypeStruct((n, TALL, WIDE, LANES), dtype)

    limits = jax.ShapeDtypeStruct((2, 3, WIDE, LANES), f32)
    m1, m2, *state = pl.pallas_call(
        assemble_kernel,
        out_shape=(strip, strip_longer, field(4), limits, limits),
        in_specs=[vmem] * 6,
        out_specs=(vmem,) * 5,
        compiler_params=params,
    )(more, a_own, a_other, side_b, far, cross)
    g2 = swapped(m2, lambda v, r, c: (v, ((r + 1) ^ 1) - 1, c), sizes)
    g1 = swapped(m1, lambda v, r, c: (v, r ^ 1, c), sizes)
    tables = [pltpu.VMEM((WIDE, LANES), f32), pltpu.VMEM((WIDE, LANES), f32), pltpu.VMEM((WIDE, LANES), jnp.int32)]
    fields = [field(2), field(2, jnp.int32)] + [field(2)] * 13
    more_state = pl.pallas_call(
        lambda *refs: inner_kernel(sizes, *refs),
        out_shape=tuple(fields),
        in_specs=[vmem] * 3,
        out_specs=(vmem,) * 15,
        scratch_shapes=tables,
        compiler_params=params,
        cost_estimate=pl.CostEstimate(flops=20_000_000, bytes_accessed=4_000_000, transcendentals=0),
    )(*state)
    state = [*state, *more_state]
    refine, dual, *_ = pl.pallas_call(
        lambda *refs: outer_kernel(sizes, *refs),
        out_shape=(
            jax.ShapeDtypeStruct((1, OUT_ROWS, BLOCKS * LANES), f32),
            jax.ShapeDtypeStruct((1, 2, OUT_ROWS, BLOCKS * LANES), f32),
            field(4),
            limits,
            limits,
            *fields,
        ),
        in_specs=[vmem] * 22,
        out_specs=(vmem,) * 20,
        input_output_aliases={4 + n: 2 + n for n in range(18)},
        scratch_shapes=[*tables, pltpu.VMEM((OUT_ROWS, BLOCKS, LANES), f32)],
        compiler_params=params,
    )(m1, m2, g1, g2, *state)
    return refine, dual


def solution(mesh):
    sizes = tuple(mesh.shape[axis] for axis in AXES)
    return jax.shard_map(
        lambda *args: on_device(sizes, *args),
        mesh=mesh,
        in_specs=(P("view", "row", "col"), P("view", "row", "col"), P("view", "row", "col", None)),
        out_specs=(P("view", "row", "col"), P("view", None, "row", "col")),
        check_vma=False,
    )
```

```python
import jax
import jax.numpy as jnp
from jax import lax
from jax.experimental import pallas as pl
from jax.experimental.pallas import tpu as pltpu
from jax.sharding import PartitionSpec as P

AXES = ("view", "row", "col")
LANES = 128
OUT_ROWS = 8
BLOCKS = 8
TILE_PACK = 17
STRIP = 30
SHIFT = 16
WIDE = 40
TALL = 16
VMEM_BYTES = 40 * 1024 * 1024

tau = 0.25
sigma = 0.5
huber_eps = 0.05
edge_gain = 2.0
slope_floor = 0.05
couple_weight = 0.5
data_weight = 1.0


def swapped(block, partner, sizes):
    views, rows, cols = sizes
    route = []
    for v in range(views):
        for r in range(rows):
            for c in range(cols):
                to_v, to_r, to_c = partner(v, r, c)
                if 0 <= to_r < rows and 0 <= to_c < cols:
                    route.append(((v * rows + r) * cols + c, (to_v * rows + to_r) * cols + to_c))
    return lax.ppermute(block, AXES, route)


def to_slabs(tile):
    parts = jnp.stack([tile[:, LANES * j : LANES * (j + 1)] for j in range(BLOCKS)])
    return jnp.transpose(parts, (1, 0, 2))


def pack_kernel(image_hbm, coarse_hbm, bounds_hbm, out_ref, longer_ref, image_ref, coarse_ref, bounds_ref, sems):
    copies = [
        pltpu.make_async_copy(source, target, sems.at[n])
        for n, (source, target) in enumerate(
            ((image_hbm, image_ref), (coarse_hbm, coarse_ref), (bounds_hbm, bounds_ref))
        )
    ]
    for copy in copies:
        copy.start()
    copies[0].wait()
    image = image_ref[0]
    slabs = to_slabs(image)
    out_ref[0:8] = slabs
    longer_ref[0:8] = slabs
    copies[1].wait()
    coarse = coarse_ref[0].astype(jnp.float32)
    slabs = to_slabs(coarse)
    out_ref[8:16] = slabs
    longer_ref[8:16] = slabs
    copies[2].wait()
    sub = lax.broadcasted_iota(jnp.int32, (BLOCKS, LANES), 0)
    limits = jnp.where(sub == 0, bounds_ref[0, 0, 0, 0], bounds_ref[0, 0, 0, 1]).astype(jnp.float32)
    out_ref[16] = limits
    longer_ref[16] = limits
    longer_ref[17] = jnp.zeros((BLOCKS, LANES), jnp.float32)


def place_kernel(own_ref, out_ref):
    out_ref[...] = own_ref[...]


def join_kernel(own_ref, other_ref, a_ref, more_ref):
    odd = (lax.axis_index("col") & 1) == 1
    more_ref[0:TILE_PACK] = own_ref[...]
    more_ref[TILE_PACK : 2 * TILE_PACK] = other_ref[0:TILE_PACK]
    for n in range(2):
        for y in range(8):
            at = 8 * n + y
            more_ref[2 * TILE_PACK + n, y : y + 1, :] = jnp.where(odd, a_ref[at, 7:8], a_ref[at, 0:1])


def near_kernel(b_ref, out_ref, thin_ref):
    odd = (lax.axis_index("col") & 1) == 1
    for n, base in enumerate((0, TILE_PACK, TILE_PACK + 8)):
        for y in range(8):
            out_ref[n, y : y + 1, :] = jnp.where(odd, b_ref[base + y, 0:1], b_ref[base + y, 7:8])
    for n in range(2):
        thin_ref[n] = b_ref[2 * TILE_PACK + n]


def halo_slabs(view):
    mid = (-5, 1) if view == 0 else (-1, 5)
    near = [(p, d) for p in (0, 1) for d in (1, 2)]
    mean = [(p, d) for p in (0, 1) for d in (3, 4)]
    slabs = [[(p, d, g, 8)] for p, d in near for g in (-5, 3)] + [[(p, d, 11, 2) for p, d in near]]
    slabs += [[(p, d, -1, 8)] for p, d in mean] + [[(p, d, 7, 2) for p, d in mean]]
    slabs += [[(p, 1, g, 8)] for p in (2, 3) for g in (-8, 0, 8)]
    slabs += [[(p, d, g, 8)] for p in (2, 3) for d in (2, 3) for g in mid]
    return slabs


def assemble_kernel(both_ref, a_own_ref, a_other_ref, b_ref, far_ref, cross_ref, m1_ref, m2_ref, F, LO, HI):
    odd = (lax.axis_index("col") & 1) == 1
    even_row = (lax.axis_index("row") & 1) == 0
    first = lax.axis_index("view") == 0
    zero = jnp.zeros((8, LANES), jnp.float32)
    m2_ref[STRIP] = zero
    for plane in range(4):
        base = (plane // 2) * TILE_PACK + (plane % 2) * 8
        a_ref = (a_own_ref, a_other_ref)[plane // 2]
        for y in range(8):
            at, a_tile = base + y, a_ref[(plane % 2) * 8 + y]
            F[plane, y + 4, 0:8] = zero
            F[plane, y + 4, 8:16] = jnp.where(odd, a_tile, b_ref[at])
            F[plane, y + 4, 16:24] = both_ref[at]
            F[plane, y + 4, 24:32] = jnp.where(odd, b_ref[at], a_tile)
            F[plane, y + 4, 32:40] = zero
    far = far_ref[...]
    near = (b_ref[2 * TILE_PACK], cross_ref[0], cross_ref[1])
    left = [jnp.where(odd, far[n], near[n]) for n in range(3)]
    right = [jnp.where(odd, near[n], far[n]) for n in range(3)]
    cross = [jnp.where(first, one, two) for one, two in zip(left, right, strict=True)]
    low, high = SHIFT - 9, SHIFT + 16
    for y in range(8):
        row = slice(y, y + 1)
        F[0, y + 4, low : low + 1] = left[0][row]
        F[0, y + 4, high : high + 1] = right[0][row]
        for plane in (2, 3):
            F[plane, y + 4, low : low + 1] = cross[plane - 1][row]
            F[plane, y + 4, high : high + 1] = cross[plane - 1][row]

    def put(at, top, bottom):
        m1_ref[at] = jnp.where(even_row, bottom, top)
        m2_ref[at] = jnp.where(even_row, top, bottom)

    def collect(pieces, row_of):
        parts = [F[plane, row_of(d), SHIFT + g : SHIFT + g + n] for plane, d, g, n in pieces]
        return parts[0] if len(parts) == 1 else jnp.concatenate(parts, axis=0)

    for at, (one, two) in enumerate(zip(halo_slabs(0), halo_slabs(1), strict=True)):
        pair = []
        for row_of in (lambda d: 3 + d, lambda d: 12 - d):
            value = collect(one, row_of)
            if one != two:
                value = jnp.where(first, value, collect(two, row_of))
            pair.append(value)
        put(at, *pair)
    for w in range(2):
        s = w * TILE_PACK + 16
        a_tile = (a_own_ref, a_other_ref)[w][16]
        tiles = (jnp.where(odd, a_tile, b_ref[s]), both_ref[s], jnp.where(odd, b_ref[s], a_tile))
        thin = [jnp.concatenate([cross[1][y : y + 1], cross[2][y : y + 1]], axis=0) for y in (0, 7)]
        ends = [jnp.concatenate([t[0:2] for t in tiles] + [t], axis=0) for t in thin]
        put(STRIP - 2 + w, *ends)
        spread_bounds(LO, HI, w, 1, ends[0])


def spread_bounds(LO, HI, w, rg, rows):
    zero = jnp.zeros((8, LANES), jnp.float32)
    for j in range(3):
        at = SHIFT - 8 + 8 * j
        LO[w, rg, at : at + 8] = jnp.broadcast_to(rows[2 * j : 2 * j + 1], (8, LANES))
        HI[w, rg, at : at + 8] = jnp.broadcast_to(rows[2 * j + 1 : 2 * j + 2], (8, LANES))
    for ref in (LO, HI):
        ref[w, rg, 0:8] = zero
        ref[w, rg, 32:40] = zero


def plans(view):
    if view == 0:
        other_wide = (((-9, -1, 4), (-8, 0, 4)), ((-5, 1), (-5, 1)), ((-5, 0), (-4, 0)))
        other_narrow = ((-5, 1), (-5, 1))
        slope_wide, slope_narrow = (-9, -1, 5), (-5, 1)
    else:
        other_wide = (((-5, 3, 8), (-4, 4, 8)), ((-1, 5), (-1, 5)), ((-1, 4), (0, 4)))
        other_narrow = ((-1, 5), (-1, 5))
        slope_wide, slope_narrow = (-5, 3, 9), (-1, 5)
    own_wide = (((-5, 3, 5), (-5, 3, 5)), ((-5, 3, 4), (-4, 4)), ((-1, 1), (-1, 1)), ((-1, 0), (0,)))
    own_narrow = ((-1, 1), (-1, 1))
    return own_wide, own_narrow, other_wide, other_narrow, slope_wide, slope_narrow


def make_steps(sizes, state, MX, CV, XG, OUT):
    (F, LO, HI, G, D, RES, SL, INV, RD, IE, UA, RA, UB, RB, XA, YA, XB, YB) = state
    _, n_row, n_col = sizes
    view, row, col = lax.axis_index("view"), lax.axis_index("row"), lax.axis_index("col")
    lane = lax.broadcasted_iota(jnp.int32, (8, LANES), 1)
    sub = lax.broadcasted_iota(jnp.int32, (8, LANES), 0)
    total = n_col * BLOCKS * LANES
    u_bufs = (F, UA, UB, UA, None)
    ubar_bufs = (F, RA, RB, RA, None)
    p_bufs = (None, (XA, YA), (XB, YB), (XA, YA), (XB, YB))
    for i in range(0, WIDE, 8):
        x = (col * BLOCKS + (i - SHIFT) + sub) * LANES
        XG[i : i + 8] = x
        valid = (x >= 0) & (x < total)
        CV[i : i + 8] = jnp.where(valid, 1.0, 0.0)
        MX[i : i + 8] = jnp.where(valid & (x + lane < total - 1), 1.0, 0.0)

    def ahead(ref, lead, i):
        here, after = ref[(*lead, pl.ds(i, 8))], ref[(*lead, pl.ds(i + 1, 8))]
        return here, pltpu.roll(jnp.where(lane == 0, after, here), LANES - 1, 1)

    def behind(ref, lead, i):
        here, before = ref[(*lead, pl.ds(i, 8))], ref[(*lead, pl.ds(i - 1, 8))]
        return here, pltpu.roll(jnp.where(lane == LANES - 1, before, here), 1, 1)

    def masks(ry):
        y = row * OUT_ROWS + ry - 4
        ok = jnp.where((y >= 0) & (y < n_row * OUT_ROWS), 1.0, 0.0)
        down = jnp.where((y >= 0) & (y < n_row * OUT_ROWS - 1), 1.0, 0.0)
        return ok, down

    def dual_step(k, w, ry, starts, ubar, p_in, p_out, stores):
        ok, down = masks(ry)
        for g in starts:
            i = g + SHIFT
            mx = MX[i : i + 8] * ok
            my = CV[i : i + 8] * down
            here_at = (w, ry, pl.ds(i, 8))
            if k == 0:
                here, right = ahead(F, (2 * w, ry), i)
                gx, gy = (right - here) * mx, (F[2 * w, ry + 1, pl.ds(i, 8)] - here) * my
                inverse = 1.0 + edge_gain * (gx * gx + gy * gy)
                ie = inverse * inverse
                stores.append((IE, here_at, ie))
            else:
                ie = IE[here_at]
            lead = (2 * w + 1, ry) if k == 0 else (w, ry)
            lead_down = (2 * w + 1, ry + 1) if k == 0 else (w, ry + 1)
            here, right = ahead(ubar, lead, i)
            gx = (right - here) * mx
            gy = (ubar[(*lead_down, pl.ds(i, 8))] - here) * my
            if k == 0:
                qx, qy = sigma * gx, sigma * gy
            else:
                qx = p_in[0][here_at] + sigma * gx
                qy = p_in[1][here_at] + sigma * gy
            qx, qy = qx * (1.0 / (1.0 + sigma * huber_eps)), qy * (1.0 / (1.0 + sigma * huber_eps))
            shrink = lax.rsqrt(jnp.maximum(1.0, (qx * qx + qy * qy) * ie))
            stores.append((p_out[0], here_at, qx * shrink))
            stores.append((p_out[1], here_at, qy * shrink))

    def primal_step(k, w, sign, ry, starts, u_in, p_out, u_out, ubar_out, stores):
        ok, _ = masks(ry)
        rg = sum(int(ry >= n) if isinstance(ry, int) else (ry >= n).astype(jnp.int32) for n in (4, 12))
        for g in starts:
            i = g + SHIFT
            here = pl.ds(i, 8)
            here_at = (w, ry, here)
            d0 = F[2 * w + 1, ry, here]
            if k == 0:
                t = lane - sign * d0.astype(jnp.int32)
                stores.append((D, here_at, t))
            else:
                t = D[here_at]
            place, hop = t & (LANES - 1), t >> 7
            picks = [hop == -sign * m for m in range(1, 5)]

            def read(ref, lead):
                value = jnp.take_along_axis(ref[(*lead, here)], place, axis=1)
                for m in range(1, 5):
                    more = jnp.take_along_axis(ref[(*lead, pl.ds(i - sign * m, 8))], place, axis=1)
                    value = jnp.where(picks[m - 1], more, value)
                return value

            if k == 0:
                residue = read(F, (2 * (1 - w), ry)) - F[2 * w, ry, here]
                slope = read(G, (1 - w, ry)) * float(-sign)
                inv = 1.0 / jnp.maximum(slope * slope, slope_floor)
                target = XG[i : i + 8] + t
                inside = (target >= 0) & (target < total)
                rden = jnp.where(inside, 1.0 / (1.0 + tau * couple_weight), 1.0)
                stores += [(RES, here_at, residue), (SL, here_at, slope), (INV, here_at, inv), (RD, here_at, rden)]
            else:
                residue, slope = RES[here_at], SL[here_at]
                inv, rden = INV[here_at], RD[here_at]
            partner = read(u_in, (2 * (1 - w) + 1, ry) if k == 0 else (1 - w, ry))
            u = d0 if k == 0 else u_in[here_at]
            px, px_left = behind(p_out[0], (w, ry), i)
            div = px - px_left + p_out[1][here_at] - p_out[1][w, ry - 1, here]
            blended = (u + tau * div + (tau * couple_weight) * partner) * rden
            mismatch = residue + slope * (blended - d0)
            limit = (data_weight * tau) * rden
            step = jnp.minimum(jnp.maximum(mismatch * inv, -limit), limit)
            new = jnp.minimum(jnp.maximum(blended - slope * step, LO[w, rg, here]), HI[w, rg, here])
            if k < 3:
                new = new * (CV[i : i + 8] * ok)
                stores.append((u_out, here_at, new))
                stores.append((ubar_out, here_at, 2.0 * new - u))
            else:
                stores.append((OUT, (ry - 4,), new - d0))

    def slope_step(w, ry, starts, stores):
        for g in starts:
            i = g + SHIFT
            _, right = ahead(F, (2 * w, ry), i)
            _, left = behind(F, (2 * w, ry), i)
            stores.append((G, (w, ry, pl.ds(i, 8)), (right - left) * 0.5))

    def dual(k, w, y, starts, stores):
        dual_step(k, w, y + 4, starts, ubar_bufs[k], p_bufs[k], p_bufs[k + 1], stores)

    def primal(k, w, y, sign, starts, stores):
        primal_step(k, w, sign, y + 4, starts, u_bufs[k], p_bufs[k + 1], u_bufs[k + 1], ubar_bufs[k + 1], stores)

    def slopes(w, y, starts, stores):
        slope_step(w, y + 4, starts, stores)

    return dual, primal, slopes


def flush(stores):
    for ref, at, value in stores:
        ref[at] = value


def by_view(run):
    view = lax.axis_index("view")

    @pl.when(view == 0)
    def _():
        run(0)

    @pl.when(view == 1)
    def _():
        run(1)


def inner_kernel(sizes, F, LO, HI, *refs):
    state, (MX, CV, XG) = (F, LO, HI, *refs[:15]), refs[15:]
    dual, primal, slopes = make_steps(sizes, state, MX, CV, XG, None)

    def run(v):
        own, _, other, _, slope_other, _ = plans(v)
        signs = (1 - 2 * v, 2 * v - 1)
        for k in range(3):
            first, last = k + 1, 7 - k

            def dual_row(y, stores, k=k):
                for w, plan in enumerate((own, other)):
                    dual(k, w, y, plan[k][0], stores)
                if k == 0:
                    slopes(0, y, (-8, 0, 8), stores)
                    slopes(1, y, slope_other, stores)

            for y in (first - 1, first):
                stores = []
                dual_row(y, stores)
                flush(stores)
            for y in range(first, last):
                stores = []
                for w, plan in enumerate((own, other)):
                    primal(k, w, y, signs[w], plan[k][1], stores)
                if y + 1 < last:
                    dual_row(y + 1, stores)
                flush(stores)
        stores = []
        slopes(0, 7, (-8, 0, 8), stores)
        slopes(1, 7, slope_other, stores)
        flush(stores)

    by_view(run)


def outer_kernel(sizes, m1_ref, m2_ref, g1_ref, g2_ref, *refs):
    refine_ref, dual_ref = refs[18:20]
    state = refs[20:38]
    MX, CV, XG, OUT = refs[38:]
    F, LO, HI = state[:3]
    XB, YB = state[16:]
    dual, primal, slopes = make_steps(sizes, state, MX, CV, XG, OUT)
    even_row = (lax.axis_index("row") & 1) == 0

    def above_below(at):
        one, two = g1_ref[at], g2_ref[at]
        return jnp.where(even_row, two, one), jnp.where(even_row, one, two)

    def run(v):
        own, own_narrow, other, other_narrow, slope_wide, slope_narrow = plans(v)
        signs = (1 - 2 * v, 2 * v - 1)
        for at, pieces in enumerate(halo_slabs(v)):
            above, below = above_below(at)
            start = 0
            for plane, d, g, n in pieces:
                F[plane, 4 - d, SHIFT + g : SHIFT + g + n] = above[start : start + n]
                F[plane, 11 + d, SHIFT + g : SHIFT + g + n] = below[start : start + n]
                start += n
        thin = SHIFT - 9 if v == 0 else SHIFT + 16
        for w in range(2):
            above, below = above_below(STRIP - 2 + w)
            spread_bounds(LO, HI, w, 0, above)
            spread_bounds(LO, HI, w, 2, below)
            if w == 0:
                for plane in (2, 3):
                    F[plane, 3, thin : thin + 1] = above[4 + plane : 5 + plane]
                    F[plane, 12, thin : thin + 1] = below[4 + plane : 5 + plane]
        stores = []
        for y in (-2, -1, 8, 9):
            slopes(0, y, (-5, 3, 5), stores)
        for y in (-1, 8):
            slopes(1, y, slope_wide, stores)
        for y in (-3, -2, 9, 10):
            slopes(1, y, slope_narrow, stores)
        flush(stores)

        def pairs(step):
            for i in range(2):
                stores = []
                step(i, stores)
                flush(stores)

        def block(step):
            stores = []
            step(stores)
            flush(stores)

        for k in range(3):
            narrow_own = own_narrow if k < 2 else own[2]
            narrow_other = other_narrow if k == 0 else other[k]
            top_o, low_o = k - 4, 9 - k
            top_n, low_n = k - 3, 8 - k

            def dual_loop(i, stores):
                for y in (top_o + i, low_o + i):
                    dual(k, 0, y, narrow_own[0], stores)
                for y in (top_n + i, low_n + i):
                    dual(k, 1, y, narrow_other[0], stores)

            def dual_block(stores):
                for y in (k - 2, k - 1, 7 - k, 8 - k):
                    dual(k, 0, y, own[k][0], stores)
                for y in (k - 1, 7 - k):
                    dual(k, 1, y, other[k][0], stores)

            def primal_loop(i, stores):
                for y in (k - 3 + i, 9 - k + i):
                    primal(k, 0, y, signs[0], narrow_own[1], stores)
                for y in (k - 2 + i, 8 - k + i):
                    primal(k, 1, y, signs[1], narrow_other[1], stores)

            def primal_block(stores):
                for y in (k - 1, k, 7 - k, 8 - k):
                    primal(k, 0, y, signs[0], own[k][1], stores)
                for y in (k, 7 - k):
                    primal(k, 1, y, signs[1], other[k][1], stores)

            pairs(dual_loop)
            block(dual_block)
            pairs(primal_loop)
            block(primal_block)

        def last_dual(i, stores):
            for y in (3 * i - 1, 3 * i, 3 * i + 1):
                dual(3, 0, y, own[3][0], stores)

        def last_primal(i, stores):
            for y in (4 * i, 4 * i + 1, 4 * i + 2, 4 * i + 3):
                primal(3, 0, y, signs[0], own[3][1], stores)

        for step, count in ((last_dual, 3), (last_primal, 2)):
            for i in range(count):
                stores = []
                step(i, stores)
                flush(stores)

    by_view(run)

    def from_slabs(slabs, put):
        parts = jnp.transpose(slabs, (1, 0, 2))
        for j in range(BLOCKS):
            put(slice(LANES * j, LANES * (j + 1)), parts[j])

    def put_refine(at, value):
        refine_ref[0, :, at] = value

    def put_x(at, value):
        dual_ref[0, 0, :, at] = value

    def put_y(at, value):
        dual_ref[0, 1, :, at] = value

    from_slabs(OUT[...], put_refine)
    from_slabs(XB[0, 4:12, SHIFT : SHIFT + 8], put_x)
    from_slabs(YB[0, 4:12, SHIFT : SHIFT + 8], put_y)


def on_device(sizes, image, coarse, bounds):
    f32 = jnp.float32
    vmem = pl.BlockSpec(memory_space=pltpu.VMEM)
    hbm = pl.BlockSpec(memory_space=pltpu.HBM)
    params = pltpu.CompilerParams(vmem_limit_bytes=VMEM_BYTES)
    tile = jax.ShapeDtypeStruct((TILE_PACK, BLOCKS, LANES), f32)
    own, longer = pl.pallas_call(
        pack_kernel,
        out_shape=(tile, jax.ShapeDtypeStruct((TILE_PACK + 1, BLOCKS, LANES), f32)),
        in_specs=[hbm] * 3,
        out_specs=(vmem, vmem),
        scratch_shapes=[
            pltpu.VMEM(image.shape, f32),
            pltpu.VMEM(coarse.shape, jnp.int32),
            pltpu.SMEM(bounds.shape, jnp.int32),
            pltpu.SemaphoreType.DMA((3,)),
        ],
    )(image, coarse, bounds)

    def in_pair(v, r, c):
        return v, r, c ^ 1

    def across(v, r, c):
        return 1 - v, r, c

    other = swapped(longer, across, sizes)
    a_own = swapped(own, in_pair, sizes)
    placed = pl.pallas_call(
        place_kernel,
        out_shape=tile,
        in_specs=[vmem],
        out_specs=vmem,
        compiler_params=params,
        cost_estimate=pl.CostEstimate(flops=4_000_000, bytes_accessed=200_000, transcendentals=0),
    )(own)
    more = pl.pallas_call(
        join_kernel,
        out_shape=jax.ShapeDtypeStruct((2 * TILE_PACK + 2, BLOCKS, LANES), f32),
        in_specs=[vmem] * 3,
        out_specs=vmem,
        compiler_params=params,
    )(placed, other, a_own)
    side_b = swapped(more, lambda v, r, c: (v, r, ((c + 1) ^ 1) - 1), sizes)
    a_other = swapped(other, in_pair, sizes)
    near, thin = pl.pallas_call(
        near_kernel,
        out_shape=(
            jax.ShapeDtypeStruct((3, BLOCKS, LANES), f32),
            jax.ShapeDtypeStruct((2, BLOCKS, LANES), f32),
        ),
        in_specs=[vmem],
        out_specs=(vmem, vmem),
        compiler_params=params,
    )(side_b)
    cross = swapped(thin, across, sizes)
    far = swapped(near, in_pair, sizes)
    strip = jax.ShapeDtypeStruct((STRIP, 8, LANES), f32)
    strip_longer = jax.ShapeDtypeStruct((STRIP + 1, 8, LANES), f32)

    def field(n, dtype=f32):
        return jax.ShapeDtypeStruct((n, TALL, WIDE, LANES), dtype)

    limits = jax.ShapeDtypeStruct((2, 3, WIDE, LANES), f32)
    m1, m2, *state = pl.pallas_call(
        assemble_kernel,
        out_shape=(strip, strip_longer, field(4), limits, limits),
        in_specs=[vmem] * 6,
        out_specs=(vmem,) * 5,
        compiler_params=params,
    )(more, a_own, a_other, side_b, far, cross)
    g2 = swapped(m2, lambda v, r, c: (v, ((r + 1) ^ 1) - 1, c), sizes)
    g1 = swapped(m1, lambda v, r, c: (v, r ^ 1, c), sizes)
    tables = [pltpu.VMEM((WIDE, LANES), f32), pltpu.VMEM((WIDE, LANES), f32), pltpu.VMEM((WIDE, LANES), jnp.int32)]
    fields = [field(2), field(2, jnp.int32)] + [field(2)] * 13
    more_state = pl.pallas_call(
        lambda *refs: inner_kernel(sizes, *refs),
        out_shape=tuple(fields),
        in_specs=[vmem] * 3,
        out_specs=(vmem,) * 15,
        scratch_shapes=tables,
        compiler_params=params,
        cost_estimate=pl.CostEstimate(flops=20_000_000, bytes_accessed=4_000_000, transcendentals=0),
    )(*state)
    state = [*state, *more_state]
    refine, dual, *_ = pl.pallas_call(
        lambda *refs: outer_kernel(sizes, *refs),
        out_shape=(
            jax.ShapeDtypeStruct((1, OUT_ROWS, BLOCKS * LANES), f32),
            jax.ShapeDtypeStruct((1, 2, OUT_ROWS, BLOCKS * LANES), f32),
            field(4),
            limits,
            limits,
            *fields,
        ),
        in_specs=[vmem] * 22,
        out_specs=(vmem,) * 20,
        input_output_aliases={4 + n: 2 + n for n in range(18)},
        scratch_shapes=[*tables, pltpu.VMEM((OUT_ROWS, BLOCKS, LANES), f32)],
        compiler_params=params,
    )(m1, m2, g1, g2, *state)
    return refine, dual


def solution(mesh):
    sizes = tuple(mesh.shape[axis] for axis in AXES)
    return jax.shard_map(
        lambda *args: on_device(sizes, *args),
        mesh=mesh,
        in_specs=(P("view", "row", "col"), P("view", "row", "col"), P("view", "row", "col", None)),
        out_specs=(P("view", "row", "col"), P("view", None, "row", "col")),
        check_vma=False,
    )
```

```python
import jax
import jax.numpy as jnp
from jax import lax
from jax.experimental import pallas as pl
from jax.experimental.pallas import tpu as pltpu
from jax.sharding import PartitionSpec as P

AXES = ("view", "row", "col")
LANES = 128
OUT_ROWS = 8
BLOCKS = 8
TILE_PACK = 17
STRIP = 30
SHIFT = 16
WIDE = 40
TALL = 16
VMEM_BYTES = 40 * 1024 * 1024

tau = 0.25
sigma = 0.5
huber_eps = 0.05
edge_gain = 2.0
slope_floor = 0.05
couple_weight = 0.5
data_weight = 1.0


def swapped(block, partner, sizes):
    views, rows, cols = sizes
    route = []
    for v in range(views):
        for r in range(rows):
            for c in range(cols):
                to_v, to_r, to_c = partner(v, r, c)
                if 0 <= to_r < rows and 0 <= to_c < cols:
                    route.append(((v * rows + r) * cols + c, (to_v * rows + to_r) * cols + to_c))
    return lax.ppermute(block, AXES, route)


def to_slabs(tile):
    parts = jnp.stack([tile[:, LANES * j : LANES * (j + 1)] for j in range(BLOCKS)])
    return jnp.transpose(parts, (1, 0, 2))


def pack_kernel(image_hbm, coarse_hbm, bounds_hbm, out_ref, longer_ref, image_ref, coarse_ref, bounds_ref, sems):
    copies = [
        pltpu.make_async_copy(source, target, sems.at[n])
        for n, (source, target) in enumerate(
            ((image_hbm, image_ref), (coarse_hbm, coarse_ref), (bounds_hbm, bounds_ref))
        )
    ]
    for copy in copies:
        copy.start()
    copies[0].wait()
    image = image_ref[0]
    slabs = to_slabs(image)
    out_ref[0:8] = slabs
    longer_ref[0:8] = slabs
    copies[1].wait()
    coarse = coarse_ref[0].astype(jnp.float32)
    slabs = to_slabs(coarse)
    out_ref[8:16] = slabs
    longer_ref[8:16] = slabs
    copies[2].wait()
    sub = lax.broadcasted_iota(jnp.int32, (BLOCKS, LANES), 0)
    limits = jnp.where(sub == 0, bounds_ref[0, 0, 0, 0], bounds_ref[0, 0, 0, 1]).astype(jnp.float32)
    out_ref[16] = limits
    longer_ref[16] = limits
    longer_ref[17] = jnp.zeros((BLOCKS, LANES), jnp.float32)


def place_kernel(own_ref, out_ref):
    out_ref[...] = own_ref[...]


def join_kernel(own_ref, other_ref, a_ref, more_ref):
    odd = (lax.axis_index("col") & 1) == 1
    more_ref[0:TILE_PACK] = own_ref[...]
    more_ref[TILE_PACK : 2 * TILE_PACK] = other_ref[0:TILE_PACK]
    for n in range(2):
        for y in range(8):
            at = 8 * n + y
            more_ref[2 * TILE_PACK + n, y : y + 1, :] = jnp.where(odd, a_ref[at, 7:8], a_ref[at, 0:1])


def near_kernel(b_ref, out_ref, thin_ref):
    odd = (lax.axis_index("col") & 1) == 1
    for n, base in enumerate((0, TILE_PACK, TILE_PACK + 8)):
        for y in range(8):
            out_ref[n, y : y + 1, :] = jnp.where(odd, b_ref[base + y, 0:1], b_ref[base + y, 7:8])
    for n in range(2):
        thin_ref[n] = b_ref[2 * TILE_PACK + n]


def halo_slabs(view):
    mid = (-5, 1) if view == 0 else (-1, 5)
    near = [(p, d) for p in (0, 1) for d in (1, 2)]
    mean = [(p, d) for p in (0, 1) for d in (3, 4)]
    slabs = [[(p, d, g, 8)] for p, d in near for g in (-5, 3)] + [[(p, d, 11, 2) for p, d in near]]
    slabs += [[(p, d, -1, 8)] for p, d in mean] + [[(p, d, 7, 2) for p, d in mean]]
    slabs += [[(p, 1, g, 8)] for p in (2, 3) for g in (-8, 0, 8)]
    slabs += [[(p, d, g, 8)] for p in (2, 3) for d in (2, 3) for g in mid]
    return slabs


def assemble_kernel(both_ref, a_own_ref, a_other_ref, b_ref, far_ref, cross_ref, m1_ref, m2_ref, F, LO, HI):
    odd = (lax.axis_index("col") & 1) == 1
    even_row = (lax.axis_index("row") & 1) == 0
    first = lax.axis_index("view") == 0
    zero = jnp.zeros((8, LANES), jnp.float32)
    m2_ref[STRIP] = zero
    for plane in range(4):
        base = (plane // 2) * TILE_PACK + (plane % 2) * 8
        a_ref = (a_own_ref, a_other_ref)[plane // 2]
        for y in range(8):
            at, a_tile = base + y, a_ref[(plane % 2) * 8 + y]
            F[plane, y + 4, 0:8] = zero
            F[plane, y + 4, 8:16] = jnp.where(odd, a_tile, b_ref[at])
            F[plane, y + 4, 16:24] = both_ref[at]
            F[plane, y + 4, 24:32] = jnp.where(odd, b_ref[at], a_tile)
            F[plane, y + 4, 32:40] = zero
    far = far_ref[...]
    near = (b_ref[2 * TILE_PACK], cross_ref[0], cross_ref[1])
    left = [jnp.where(odd, far[n], near[n]) for n in range(3)]
    right = [jnp.where(odd, near[n], far[n]) for n in range(3)]
    cross = [jnp.where(first, one, two) for one, two in zip(left, right, strict=True)]
    low, high = SHIFT - 9, SHIFT + 16
    for y in range(8):
        row = slice(y, y + 1)
        F[0, y + 4, low : low + 1] = left[0][row]
        F[0, y + 4, high : high + 1] = right[0][row]
        for plane in (2, 3):
            F[plane, y + 4, low : low + 1] = cross[plane - 1][row]
            F[plane, y + 4, high : high + 1] = cross[plane - 1][row]

    def put(at, top, bottom):
        m1_ref[at] = jnp.where(even_row, bottom, top)
        m2_ref[at] = jnp.where(even_row, top, bottom)

    def collect(pieces, row_of):
        parts = [F[plane, row_of(d), SHIFT + g : SHIFT + g + n] for plane, d, g, n in pieces]
        return parts[0] if len(parts) == 1 else jnp.concatenate(parts, axis=0)

    for at, (one, two) in enumerate(zip(halo_slabs(0), halo_slabs(1), strict=True)):
        pair = []
        for row_of in (lambda d: 3 + d, lambda d: 12 - d):
            value = collect(one, row_of)
            if one != two:
                value = jnp.where(first, value, collect(two, row_of))
            pair.append(value)
        put(at, *pair)
    for w in range(2):
        s = w * TILE_PACK + 16
        a_tile = (a_own_ref, a_other_ref)[w][16]
        tiles = (jnp.where(odd, a_tile, b_ref[s]), both_ref[s], jnp.where(odd, b_ref[s], a_tile))
        thin = [jnp.concatenate([cross[1][y : y + 1], cross[2][y : y + 1]], axis=0) for y in (0, 7)]
        ends = [jnp.concatenate([t[0:2] for t in tiles] + [t], axis=0) for t in thin]
        put(STRIP - 2 + w, *ends)
        spread_bounds(LO, HI, w, 1, ends[0])


def spread_bounds(LO, HI, w, rg, rows):
    zero = jnp.zeros((8, LANES), jnp.float32)
    for j in range(3):
        at = SHIFT - 8 + 8 * j
        LO[w, rg, at : at + 8] = jnp.broadcast_to(rows[2 * j : 2 * j + 1], (8, LANES))
        HI[w, rg, at : at + 8] = jnp.broadcast_to(rows[2 * j + 1 : 2 * j + 2], (8, LANES))
    for ref in (LO, HI):
        ref[w, rg, 0:8] = zero
        ref[w, rg, 32:40] = zero


def plans(view):
    if view == 0:
        other_wide = (((-9, -1, 4), (-8, 0, 4)), ((-5, 1), (-5, 1)), ((-5, 0), (-4, 0)))
        other_narrow = ((-5, 1), (-5, 1))
        slope_wide, slope_narrow = (-9, -1, 5), (-5, 1)
    else:
        other_wide = (((-5, 3, 8), (-4, 4, 8)), ((-1, 5), (-1, 5)), ((-1, 4), (0, 4)))
        other_narrow = ((-1, 5), (-1, 5))
        slope_wide, slope_narrow = (-5, 3, 9), (-1, 5)
    own_wide = (((-5, 3, 5), (-5, 3, 5)), ((-5, 3, 4), (-4, 4)), ((-1, 1), (-1, 1)), ((-1, 0), (0,)))
    own_narrow = ((-1, 1), (-1, 1))
    return own_wide, own_narrow, other_wide, other_narrow, slope_wide, slope_narrow


def make_steps(sizes, state, MX, CV, XG, OUT):
    (F, LO, HI, G, D, RES, SL, INV, RD, IE, UA, RA, UB, RB, XA, YA, XB, YB) = state
    _, n_row, n_col = sizes
    view, row, col = lax.axis_index("view"), lax.axis_index("row"), lax.axis_index("col")
    lane = lax.broadcasted_iota(jnp.int32, (8, LANES), 1)
    sub = lax.broadcasted_iota(jnp.int32, (8, LANES), 0)
    total = n_col * BLOCKS * LANES
    u_bufs = (F, UA, UB, UA, None)
    ubar_bufs = (F, RA, RB, RA, None)
    p_bufs = (None, (XA, YA), (XB, YB), (XA, YA), (XB, YB))
    for i in range(0, WIDE, 8):
        x = (col * BLOCKS + (i - SHIFT) + sub) * LANES
        XG[i : i + 8] = x
        valid = (x >= 0) & (x < total)
        CV[i : i + 8] = jnp.where(valid, 1.0, 0.0)
        MX[i : i + 8] = jnp.where(valid & (x + lane < total - 1), 1.0, 0.0)

    def ahead(ref, lead, i):
        here, after = ref[(*lead, pl.ds(i, 8))], ref[(*lead, pl.ds(i + 1, 8))]
        return here, pltpu.roll(jnp.where(lane == 0, after, here), LANES - 1, 1)

    def behind(ref, lead, i):
        here, before = ref[(*lead, pl.ds(i, 8))], ref[(*lead, pl.ds(i - 1, 8))]
        return here, pltpu.roll(jnp.where(lane == LANES - 1, before, here), 1, 1)

    def masks(ry):
        y = row * OUT_ROWS + ry - 4
        ok = jnp.where((y >= 0) & (y < n_row * OUT_ROWS), 1.0, 0.0)
        down = jnp.where((y >= 0) & (y < n_row * OUT_ROWS - 1), 1.0, 0.0)
        return ok, down

    def dual_step(k, w, ry, starts, ubar, p_in, p_out, stores):
        ok, down = masks(ry)
        for g in starts:
            i = g + SHIFT
            mx = MX[i : i + 8] * ok
            my = CV[i : i + 8] * down
            here_at = (w, ry, pl.ds(i, 8))
            if k == 0:
                here, right = ahead(F, (2 * w, ry), i)
                gx, gy = (right - here) * mx, (F[2 * w, ry + 1, pl.ds(i, 8)] - here) * my
                inverse = 1.0 + edge_gain * (gx * gx + gy * gy)
                ie = inverse * inverse
                stores.append((IE, here_at, ie))
            else:
                ie = IE[here_at]
            lead = (2 * w + 1, ry) if k == 0 else (w, ry)
            lead_down = (2 * w + 1, ry + 1) if k == 0 else (w, ry + 1)
            here, right = ahead(ubar, lead, i)
            gx = (right - here) * mx
            gy = (ubar[(*lead_down, pl.ds(i, 8))] - here) * my
            if k == 0:
                qx, qy = sigma * gx, sigma * gy
            else:
                qx = p_in[0][here_at] + sigma * gx
                qy = p_in[1][here_at] + sigma * gy
            qx, qy = qx * (1.0 / (1.0 + sigma * huber_eps)), qy * (1.0 / (1.0 + sigma * huber_eps))
            shrink = lax.rsqrt(jnp.maximum(1.0, (qx * qx + qy * qy) * ie))
            stores.append((p_out[0], here_at, qx * shrink))
            stores.append((p_out[1], here_at, qy * shrink))

    def primal_step(k, w, sign, ry, starts, u_in, p_out, u_out, ubar_out, stores, part):
        ok, _ = masks(ry)
        rg = sum(int(ry >= n) if isinstance(ry, int) else (ry >= n).astype(jnp.int32) for n in (4, 12))
        for g in starts:
            i = g + SHIFT
            here = pl.ds(i, 8)
            here_at = (w, ry, here)
            d0 = F[2 * w + 1, ry, here]
            if k == 0 and part != "finish":
                t = lane - sign * d0.astype(jnp.int32)
                stores.append((D, here_at, t))
            else:
                t = D[here_at]
            place, hop = t & (LANES - 1), t >> 7
            picks = [hop == -sign * m for m in range(1, 5)]

            def read(ref, lead):
                value = jnp.take_along_axis(ref[(*lead, here)], place, axis=1)
                for m in range(1, 5):
                    more = jnp.take_along_axis(ref[(*lead, pl.ds(i - sign * m, 8))], place, axis=1)
                    value = jnp.where(picks[m - 1], more, value)
                return value

            if k == 0 and part != "finish":
                residue = read(F, (2 * (1 - w), ry)) - F[2 * w, ry, here]
                slope = read(G, (1 - w, ry)) * float(-sign)
                inv = 1.0 / jnp.maximum(slope * slope, slope_floor)
                target = XG[i : i + 8] + t
                inside = (target >= 0) & (target < total)
                rden = jnp.where(inside, 1.0 / (1.0 + tau * couple_weight), 1.0)
                stores += [(RES, here_at, residue), (SL, here_at, slope), (INV, here_at, inv), (RD, here_at, rden)]
            else:
                residue, slope = RES[here_at], SL[here_at]
                inv, rden = INV[here_at], RD[here_at]
            if part == "prepare":
                continue
            partner = read(u_in, (2 * (1 - w) + 1, ry) if k == 0 else (1 - w, ry))
            u = d0 if k == 0 else u_in[here_at]
            px, px_left = behind(p_out[0], (w, ry), i)
            div = px - px_left + p_out[1][here_at] - p_out[1][w, ry - 1, here]
            blended = (u + tau * div + (tau * couple_weight) * partner) * rden
            mismatch = residue + slope * (blended - d0)
            limit = (data_weight * tau) * rden
            step = jnp.minimum(jnp.maximum(mismatch * inv, -limit), limit)
            new = jnp.minimum(jnp.maximum(blended - slope * step, LO[w, rg, here]), HI[w, rg, here])
            if k < 3:
                new = new * (CV[i : i + 8] * ok)
                stores.append((u_out, here_at, new))
                stores.append((ubar_out, here_at, 2.0 * new - u))
            else:
                stores.append((OUT, (ry - 4,), new - d0))

    def slope_step(w, ry, starts, stores):
        for g in starts:
            i = g + SHIFT
            _, right = ahead(F, (2 * w, ry), i)
            _, left = behind(F, (2 * w, ry), i)
            stores.append((G, (w, ry, pl.ds(i, 8)), (right - left) * 0.5))

    def dual(k, w, y, starts, stores):
        dual_step(k, w, y + 4, starts, ubar_bufs[k], p_bufs[k], p_bufs[k + 1], stores)

    def primal(k, w, y, sign, starts, stores, part="whole"):
        primal_step(k, w, sign, y + 4, starts, u_bufs[k], p_bufs[k + 1], u_bufs[k + 1], ubar_bufs[k + 1], stores, part)

    def slopes(w, y, starts, stores):
        slope_step(w, y + 4, starts, stores)

    return dual, primal, slopes


def flush(stores):
    for ref, at, value in stores:
        ref[at] = value


def by_view(run):
    view = lax.axis_index("view")

    @pl.when(view == 0)
    def _():
        run(0)

    @pl.when(view == 1)
    def _():
        run(1)


def inner_kernel(sizes, F, LO, HI, *refs):
    state, (MX, CV, XG) = (F, LO, HI, *refs[:15]), refs[15:]
    dual, primal, slopes = make_steps(sizes, state, MX, CV, XG, None)

    def run(v):
        own, _, other, _, slope_other, _ = plans(v)
        signs = (1 - 2 * v, 2 * v - 1)
        for k in range(3):
            first, last = k + 1, 7 - k

            def dual_row(y, stores, k=k):
                for w, plan in enumerate((own, other)):
                    dual(k, w, y, plan[k][0], stores)
                if k == 0:
                    slopes(0, y, (-8, 0, 8), stores)
                    slopes(1, y, slope_other, stores)

            for y in (first - 1, first):
                stores = []
                dual_row(y, stores)
                flush(stores)
            for y in range(first, last):
                stores = []
                for w, plan in enumerate((own, other)):
                    primal(k, w, y, signs[w], plan[k][1], stores)
                if y + 1 < last:
                    dual_row(y + 1, stores)
                flush(stores)
        stores = []
        slopes(0, 7, (-8, 0, 8), stores)
        slopes(1, 7, slope_other, stores)
        flush(stores)
        stores = []
        for y in (0, 7):
            for w, plan in enumerate((own, other)):
                primal(0, w, y, signs[w], plan[0][1], stores, "prepare")
        dual(3, 0, 3, own[3][0], stores)
        flush(stores)

    by_view(run)


def outer_kernel(sizes, m1_ref, m2_ref, g1_ref, g2_ref, *refs):
    refine_ref, dual_ref = refs[18:20]
    state = refs[20:38]
    MX, CV, XG, OUT, flat_refine, flat_dual, sems = refs[38:]
    F, LO, HI = state[:3]
    XB, YB = state[16:]
    dual, primal, slopes = make_steps(sizes, state, MX, CV, XG, OUT)
    even_row = (lax.axis_index("row") & 1) == 0

    def above_below(at):
        one, two = g1_ref[at], g2_ref[at]
        return jnp.where(even_row, two, one), jnp.where(even_row, one, two)

    send_dual = pltpu.make_async_copy(flat_dual, dual_ref.at[0], sems.at[0])
    send_refine = pltpu.make_async_copy(flat_refine, refine_ref.at[0], sems.at[1])

    def run(v):
        own, own_narrow, other, other_narrow, slope_wide, slope_narrow = plans(v)
        signs = (1 - 2 * v, 2 * v - 1)
        for at, pieces in enumerate(halo_slabs(v)):
            above, below = above_below(at)
            start = 0
            for plane, d, g, n in pieces:
                F[plane, 4 - d, SHIFT + g : SHIFT + g + n] = above[start : start + n]
                F[plane, 11 + d, SHIFT + g : SHIFT + g + n] = below[start : start + n]
                start += n
        thin = SHIFT - 9 if v == 0 else SHIFT + 16
        for w in range(2):
            above, below = above_below(STRIP - 2 + w)
            spread_bounds(LO, HI, w, 0, above)
            spread_bounds(LO, HI, w, 2, below)
            if w == 0:
                for plane in (2, 3):
                    F[plane, 3, thin : thin + 1] = above[4 + plane : 5 + plane]
                    F[plane, 12, thin : thin + 1] = below[4 + plane : 5 + plane]
        stores = []
        for y in (-2, -1, 8, 9):
            slopes(0, y, (-5, 3, 5), stores)
        for y in (-1, 8):
            slopes(1, y, slope_wide, stores)
        for y in (-3, -2, 9, 10):
            slopes(1, y, slope_narrow, stores)
        flush(stores)

        def pairs(step):
            for i in range(2):
                stores = []
                step(i, stores)
                flush(stores)

        def block(step):
            stores = []
            step(stores)
            flush(stores)

        for k in range(3):
            narrow_own = own_narrow if k < 2 else own[2]
            narrow_other = other_narrow if k == 0 else other[k]
            top_o, low_o = k - 4, 9 - k
            top_n, low_n = k - 3, 8 - k

            def dual_loop(i, stores):
                for y in (top_o + i, low_o + i):
                    dual(k, 0, y, narrow_own[0], stores)
                for y in (top_n + i, low_n + i):
                    dual(k, 1, y, narrow_other[0], stores)

            def dual_block(stores):
                for y in (k - 2, k - 1, 7 - k, 8 - k):
                    dual(k, 0, y, own[k][0], stores)
                for y in (k - 1, 7 - k):
                    dual(k, 1, y, other[k][0], stores)

            def primal_loop(i, stores):
                for y in (k - 3 + i, 9 - k + i):
                    primal(k, 0, y, signs[0], narrow_own[1], stores)
                for y in (k - 2 + i, 8 - k + i):
                    primal(k, 1, y, signs[1], narrow_other[1], stores)

            def primal_block(stores):
                ready = "finish" if k == 0 else "whole"
                for y in (k - 1, k, 7 - k, 8 - k):
                    primal(k, 0, y, signs[0], own[k][1], stores, ready if 0 <= y < 8 else "whole")
                for y in (k, 7 - k):
                    primal(k, 1, y, signs[1], other[k][1], stores, ready)

            pairs(dual_loop)
            block(dual_block)
            pairs(primal_loop)
            block(primal_block)

        def last_dual(i, stores):
            for y in ((-1, 0, 1, 2), (4, 5, 6, 7))[i]:
                dual(3, 0, y, own[3][0], stores)

        def last_primal(i, stores):
            for y in (4 * i, 4 * i + 1, 4 * i + 2, 4 * i + 3):
                primal(3, 0, y, signs[0], own[3][1], stores)

        def flatten(slabs, put):
            parts = jnp.transpose(slabs, (1, 0, 2))
            for j in range(BLOCKS):
                put(slice(LANES * j, LANES * (j + 1)), parts[j])

        def put_refine(at, value):
            flat_refine[:, at] = value

        def put_x(at, value):
            flat_dual[0, :, at] = value

        def put_y(at, value):
            flat_dual[1, :, at] = value

        for i in range(2):
            stores = []
            last_dual(i, stores)
            flush(stores)
        flatten(XB[0, 4:12, SHIFT : SHIFT + 8], put_x)
        flatten(YB[0, 4:12, SHIFT : SHIFT + 8], put_y)
        send_dual.start()
        for i in range(2):
            stores = []
            last_primal(i, stores)
            flush(stores)
        flatten(OUT[...], put_refine)
        send_refine.start()
        send_dual.wait()
        send_refine.wait()

    by_view(run)


def on_device(sizes, image, coarse, bounds):
    f32 = jnp.float32
    vmem = pl.BlockSpec(memory_space=pltpu.VMEM)
    hbm = pl.BlockSpec(memory_space=pltpu.HBM)
    params = pltpu.CompilerParams(vmem_limit_bytes=VMEM_BYTES)
    tile = jax.ShapeDtypeStruct((TILE_PACK, BLOCKS, LANES), f32)
    own, longer = pl.pallas_call(
        pack_kernel,
        out_shape=(tile, jax.ShapeDtypeStruct((TILE_PACK + 1, BLOCKS, LANES), f32)),
        in_specs=[hbm] * 3,
        out_specs=(vmem, vmem),
        scratch_shapes=[
            pltpu.VMEM(image.shape, f32),
            pltpu.VMEM(coarse.shape, jnp.int32),
            pltpu.SMEM(bounds.shape, jnp.int32),
            pltpu.SemaphoreType.DMA((3,)),
        ],
    )(image, coarse, bounds)

    def in_pair(v, r, c):
        return v, r, c ^ 1

    def across(v, r, c):
        return 1 - v, r, c

    other = swapped(longer, across, sizes)
    a_own = swapped(own, in_pair, sizes)
    placed = pl.pallas_call(
        place_kernel,
        out_shape=tile,
        in_specs=[vmem],
        out_specs=vmem,
        compiler_params=params,
        cost_estimate=pl.CostEstimate(flops=4_000_000, bytes_accessed=200_000, transcendentals=0),
    )(own)
    more = pl.pallas_call(
        join_kernel,
        out_shape=jax.ShapeDtypeStruct((2 * TILE_PACK + 2, BLOCKS, LANES), f32),
        in_specs=[vmem] * 3,
        out_specs=vmem,
        compiler_params=params,
    )(placed, other, a_own)
    side_b = swapped(more, lambda v, r, c: (v, r, ((c + 1) ^ 1) - 1), sizes)
    a_other = swapped(other, in_pair, sizes)
    near, thin = pl.pallas_call(
        near_kernel,
        out_shape=(
            jax.ShapeDtypeStruct((3, BLOCKS, LANES), f32),
            jax.ShapeDtypeStruct((2, BLOCKS, LANES), f32),
        ),
        in_specs=[vmem],
        out_specs=(vmem, vmem),
        compiler_params=params,
    )(side_b)
    cross = swapped(thin, across, sizes)
    far = swapped(near, in_pair, sizes)
    strip = jax.ShapeDtypeStruct((STRIP, 8, LANES), f32)
    strip_longer = jax.ShapeDtypeStruct((STRIP + 1, 8, LANES), f32)

    def field(n, dtype=f32):
        return jax.ShapeDtypeStruct((n, TALL, WIDE, LANES), dtype)

    limits = jax.ShapeDtypeStruct((2, 3, WIDE, LANES), f32)
    m1, m2, *state = pl.pallas_call(
        assemble_kernel,
        out_shape=(strip, strip_longer, field(4), limits, limits),
        in_specs=[vmem] * 6,
        out_specs=(vmem,) * 5,
        compiler_params=params,
    )(more, a_own, a_other, side_b, far, cross)
    g2 = swapped(m2, lambda v, r, c: (v, ((r + 1) ^ 1) - 1, c), sizes)
    g1 = swapped(m1, lambda v, r, c: (v, r ^ 1, c), sizes)
    tables = [pltpu.VMEM((WIDE, LANES), f32), pltpu.VMEM((WIDE, LANES), f32), pltpu.VMEM((WIDE, LANES), jnp.int32)]
    fields = [field(2), field(2, jnp.int32)] + [field(2)] * 13
    more_state = pl.pallas_call(
        lambda *refs: inner_kernel(sizes, *refs),
        out_shape=tuple(fields),
        in_specs=[vmem] * 3,
        out_specs=(vmem,) * 15,
        scratch_shapes=tables,
        compiler_params=params,
        cost_estimate=pl.CostEstimate(flops=20_000_000, bytes_accessed=4_000_000, transcendentals=0),
    )(*state)
    state = [*state, *more_state]
    refine, dual, *_ = pl.pallas_call(
        lambda *refs: outer_kernel(sizes, *refs),
        out_shape=(
            jax.ShapeDtypeStruct((1, OUT_ROWS, BLOCKS * LANES), f32),
            jax.ShapeDtypeStruct((1, 2, OUT_ROWS, BLOCKS * LANES), f32),
            field(4),
            limits,
            limits,
            *fields,
        ),
        in_specs=[vmem] * 22,
        out_specs=(hbm, hbm) + (vmem,) * 18,
        input_output_aliases={4 + n: 2 + n for n in range(18)},
        scratch_shapes=[
            *tables,
            pltpu.VMEM((OUT_ROWS, BLOCKS, LANES), f32),
            pltpu.VMEM((OUT_ROWS, BLOCKS * LANES), f32),
            pltpu.VMEM((2, OUT_ROWS, BLOCKS * LANES), f32),
            pltpu.SemaphoreType.DMA((2,)),
        ],
        compiler_params=params,
    )(m1, m2, g1, g2, *state)
    return refine, dual


def solution(mesh):
    sizes = tuple(mesh.shape[axis] for axis in AXES)
    return jax.shard_map(
        lambda *args: on_device(sizes, *args),
        mesh=mesh,
        in_specs=(P("view", "row", "col"), P("view", "row", "col"), P("view", "row", "col", None)),
        out_specs=(P("view", "row", "col"), P("view", None, "row", "col")),
        check_vma=False,
    )
```
